1024 devices in a mesh: gx: 16 (over y_lo, x, core), gy: 64 (over y_hi, z).
Axes of the slice: x: 4, y: 8 (y_hi: 4, y_lo: 2; y = y_hi * 2 + y_lo), z: 16, core: 2. Of those that a mesh axis runs over, the one named last changes fastest.
Arguments:
- features: bfloat16 [32, 512, 8, 9, 128], P('gx', 'gy'), may hold values from -6 to 6
- positions: float32 [3, 32, 512, 8], P(None, 'gx', 'gy'), may hold values from 0.5 to 4.5, as said below
- occupied: int32 [32, 512, 8], P('gx', 'gy'), may hold values 0 or 1
- neighbours: int32 [32, 512, 8, 32], P('gx', 'gy'), may hold values from 0 to 72, as said below
- radial_weight: float32 [7, 8, 128], replicated, may hold values from -0.5 to 0.5
- mix_weight: bfloat16 [128, 128], replicated, may hold values from -0.5 to 0.5
- out_weight: float32 [128], replicated, may hold values from -1 to 1
Outputs:
- forces: float32 [3, 32, 512, 8], P(None, 'gx', 'gy')
- slot_energy_values: float32 [32, 512, 8], P('gx', 'gy')
- total_energy: float32 [], replicated
The draws below stay inside these ranges and needn't reach their ends.
Inputs may be any that keep to these rules, and one draw needn't show every extreme that they name: `positions`: any two atoms that a list pairs are 1 angstrom or more apart, also across cells. `neighbours`: codes as in the reference program; an atom never lists itself; the used entries of a list come first, 16 or more of them, the rest are 72.
All inputs are finite; a program needn't handle non-finite values. No bound on the sum of `occupied` on one device may be relied on, other than what follows from the above.
Results may differ from the reference program's by a relative error of at most 0.0045.
Values may be sent and summed in bfloat16 or wider, within the bound.
No kernel may reach another device: no remote copies, remote signals or barrier semaphores. Data moves between devices by JAX's collectives and lax.ppermute only.
A program may use at most 32 MiB of HBM per device.

```python
import math
import jax
import jax.numpy as jnp
import numpy as np
from jax import lax

CHANNEL_COUNT = 128
NB = 8
NEIGHBOUR_SLOTS = 32
CELL_ATOM_SLOTS = 8
SLAB_CELL_COLUMNS = 32
SLAB_CELL_ROWS = 512


def draw_positions(key, part):
    key = jax.random.fold_in(key, 11)
    slot_ids = jnp.arange(CELL_ATOM_SLOTS)
    site_x = (0.25 + 0.5 * (slot_ids % 2).astype(jnp.float32)) * 5.0
    site_y = (0.25 + 0.5 * (slot_ids // 2 % 2).astype(jnp.float32)) * 5.0
    site_z = (0.5 + (slot_ids // 4).astype(jnp.float32)) * 2.5
    lattice = jnp.stack([site_x, site_y, site_z], axis=0).astype(jnp.float32)
    random_displacement = jax.random.uniform(key, (3, SLAB_CELL_COLUMNS, SLAB_CELL_ROWS, CELL_ATOM_SLOTS), jnp.float32, -0.75, 0.75)
    return lattice[:, None, None, :] + random_displacement


def draw_neighbours(key, part):
    key = jax.random.fold_in(key, 12)
    score_random_key, count_random_key = jax.random.split(key)
    candidate_sites = 9 * CELL_ATOM_SLOTS - 1
    site_scores = jax.random.randint(score_random_key, (SLAB_CELL_COLUMNS, SLAB_CELL_ROWS, CELL_ATOM_SLOTS, candidate_sites), 0, 1048576) * 128 + jnp.arange(candidate_sites)
    order_ids = jnp.argsort(site_scores, axis=-1)[..., :NEIGHBOUR_SLOTS].astype(jnp.int32)
    own_code = (4 * CELL_ATOM_SLOTS + jnp.arange(CELL_ATOM_SLOTS, dtype=jnp.int32))[None, None, :, None]
    chosen = order_ids + (order_ids >= own_code).astype(jnp.int32)
    occupied_count = jax.random.randint(count_random_key, (SLAB_CELL_COLUMNS, SLAB_CELL_ROWS, CELL_ATOM_SLOTS, 1), NEIGHBOUR_SLOTS // 2, NEIGHBOUR_SLOTS + 1)
    return jnp.where(jnp.arange(NEIGHBOUR_SLOTS)[None, None, None, :] < occupied_count, chosen, 9 * CELL_ATOM_SLOTS).astype(jnp.int32)


def touch_ends(values, key, least, top_value):
    longest = values.shape.index(max(values.shape))
    spots = []
    for shift in (0, 1):
        where = [jax.random.randint(jax.random.fold_in(key, axis), (), 0, length) for axis, length in enumerate(values.shape)]
        where[longest] = (where[longest] + shift) % values.shape[longest]
        spots.append(tuple(where))
    return values.at[spots[0]].set(least).at[spots[1]].set(top_value)


def levels(rng, shape, cuts, least, top_value):
    factor_of = 1.0
    for dim, shards_of in cuts:
        heights = jax.random.uniform(jax.random.fold_in(jax.random.fold_in(rng, 6), dim), (shards_of,), jnp.float32, least / len(cuts), top_value / len(cuts))
        factor_of = factor_of * jnp.repeat(jnp.exp(heights), shape[dim] // shards_of).reshape((-1,) + (1,) * (len(shape) - 1 - dim))
    return factor_of


def scatter_about(own_key, extent, width, most, shards=(), kind=jnp.bfloat16):
    values = jax.random.normal(own_key, extent, jnp.float32) * width
    if len(shards) > 0:
        values = levels(own_key, extent, shards, -0.22, 0.18) * values
    return jnp.clip(values, min=-most, max=most).astype(kind)


def setup_inputs(seed: int = 0) -> dict:
    seeds = jax.random.split(jax.random.key(seed), 8)
    features = scatter_about(seeds[0], (SLAB_CELL_COLUMNS, SLAB_CELL_ROWS, CELL_ATOM_SLOTS, 9, CHANNEL_COUNT), 1.0, 6.0, ((0, 16), (1, 64)))
    positions = draw_positions(jax.random.fold_in(seeds[7], 71), 0)
    occupied = touch_ends((jax.random.randint(seeds[2], (SLAB_CELL_COLUMNS, SLAB_CELL_ROWS, CELL_ATOM_SLOTS), 0, 10) < 9).astype(jnp.int32), jax.random.fold_in(seeds[2], 1), 0, 1)
    neighbours = draw_neighbours(jax.random.fold_in(seeds[7], 71), 0)
    radial_weight = scatter_about(seeds[4], (7, NB, CHANNEL_COUNT), (NB * NEIGHBOUR_SLOTS // 2) ** -0.5, 0.5, (), jnp.float32)
    mix_weight = scatter_about(seeds[5], (CHANNEL_COUNT, CHANNEL_COUNT), CHANNEL_COUNT ** -0.5, 0.5)
    out_weight = scatter_about(seeds[6], (CHANNEL_COUNT,), (CHANNEL_COUNT // 4) ** -0.5, 1.0, (), jnp.float32)
    return {"features": features, "positions": positions, "occupied": occupied, "neighbours": neighbours, "radial_weight": radial_weight, "mix_weight": mix_weight, "out_weight": out_weight}


CELL_SIDE = 5.0
CUTOFF = 5.0
LEAD_PATHS = np.array([0, 3, 3, 3, 5, 5, 5, 5, 5], dtype=np.int32)
PLAIN_PATHS = np.array([4, 4, 4, 6, 6, 6, 6, 6], dtype=np.int32)
PAIRED_PATHS = np.array([1, 1, 1, 2, 2, 2, 2, 2], dtype=np.int32)

def edge_terms(vectors):
    dist_sq = lax.optimization_barrier(jnp.sum(vectors * vectors, axis=-1))
    distance = jnp.sqrt(dist_sq)
    unit_x = vectors[..., 0] / distance
    unit_y = vectors[..., 1] / distance
    unit_z = vectors[..., 2] / distance
    envelope = jnp.square(jnp.maximum(1.0 - dist_sq / (CUTOFF * CUTOFF), 0.0))
    orders = jnp.arange(1, NB + 1).astype(jnp.float32)
    radial = jnp.sin(orders * (math.pi / CUTOFF) * distance[..., None]) / distance[..., None] * envelope[..., None]
    root3 = math.sqrt(3.0)
    root15 = math.sqrt(15.0)
    root5 = math.sqrt(5.0)
    harmonics = jnp.stack([jnp.ones_like(unit_x), root3 * unit_x, root3 * unit_y, root3 * unit_z, root15 * unit_x * unit_y, root15 * unit_y * unit_z, 0.5 * root5 * (3.0 * unit_z * unit_z - 1.0), root15 * unit_x * unit_z, 0.5 * root15 * (unit_x * unit_x - unit_y * unit_y)], axis=-1)
    return radial[..., :, None] * harmonics[..., None, :]

def block_step(neigh_rows, vectors, weights, own_occupied, radial_weight, mix_weight, out_weight):
    highest = lax.Precision.HIGHEST

    def geometry_of(edge_vectors):
        return edge_terms(edge_vectors) * weights[..., None, None]
    geometry, pull_back = jax.vjp(geometry_of, vectors)
    rounded = geometry.astype(jnp.bfloat16).astype(jnp.float32)
    neigh_f32 = neigh_rows.astype(jnp.float32)
    lead_sum = jnp.einsum('akbg,akc->abgc', rounded, neigh_f32[:, :, 0], precision=highest)
    plain_sum = jnp.einsum('akb,akmc->abmc', rounded[..., 0], neigh_f32[:, :, 1:], precision=highest)
    paired_sum = jnp.einsum('akbm,akmc->abmc', rounded[..., 1:], neigh_f32[:, :, 1:], precision=highest)
    w_lead = radial_weight[LEAD_PATHS]
    w_plain = radial_weight[PLAIN_PATHS]
    w_paired = radial_weight[PAIRED_PATHS]
    part_lead = jnp.einsum('abgc,gbc->agc', lead_sum, w_lead, precision=highest)
    part_plain = jnp.einsum('abmc,mbc->amc', plain_sum, w_plain, precision=highest)
    part_paired = jnp.einsum('abmc,mbc->ac', paired_sum, w_paired, precision=highest)
    messages = part_lead + jnp.concatenate([part_paired[:, None], part_plain], axis=1)
    messages = messages.astype(jnp.bfloat16)
    mixed_out = jnp.einsum('agc,cd->agd', messages.astype(jnp.float32), mix_weight.astype(jnp.float32), precision=highest)
    pre_act = mixed_out[:, 0] + lax.optimization_barrier(jnp.sum(mixed_out[:, 1:] * mixed_out[:, 1:], axis=1))
    gate_value = jax.nn.sigmoid(pre_act)
    energy_values = own_occupied * jnp.dot(pre_act * gate_value, out_weight, precision=highest)
    grad_z = own_occupied[:, None] * out_weight[None, :] * gate_value * (1.0 + pre_act * (1.0 - gate_value))
    grad_mixed = jnp.concatenate([grad_z[:, None], 2.0 * grad_z[:, None] * mixed_out[:, 1:]], axis=1)
    grad_mixed = grad_mixed.astype(jnp.bfloat16)
    grad_messages = jnp.einsum('agd,cd->agc', grad_mixed.astype(jnp.float32), mix_weight.astype(jnp.float32), precision=highest)
    grad_lead = (jnp.transpose(w_lead, (1, 0, 2))[None] * grad_messages[:, None]).astype(jnp.bfloat16)
    grad_plain = (jnp.transpose(w_plain, (1, 0, 2))[None] * grad_messages[:, None, 1:]).astype(jnp.bfloat16)
    grad_paired = (jnp.transpose(w_paired, (1, 0, 2))[None] * grad_messages[:, None, None, 0]).astype(jnp.bfloat16)
    grad_all = jnp.einsum('abgc,akc->akbg', grad_lead.astype(jnp.float32), neigh_f32[:, :, 0], precision=highest)
    grad_zero = jnp.einsum('abmc,akmc->akb', grad_plain.astype(jnp.float32), neigh_f32[:, :, 1:], precision=highest)
    grad_rest = jnp.einsum('abmc,akmc->akbm', grad_paired.astype(jnp.float32), neigh_f32[:, :, 1:], precision=highest)
    grad_geometry = grad_all + jnp.concatenate([grad_zero[..., None], grad_rest], axis=-1)
    edge_gradient = pull_back(grad_geometry)[0]
    return (energy_values, edge_gradient)

def reference(features, positions, occupied, neighbours, radial_weight, mix_weight, out_weight):
    summed_atom_energy = SLAB_CELL_COLUMNS * SLAB_CELL_ROWS * CELL_ATOM_SLOTS
    block_cells = math.gcd(SLAB_CELL_ROWS, 8)
    blocks_per_row = SLAB_CELL_ROWS // block_cells
    feat_rows = features.reshape(summed_atom_energy, 9, CHANNEL_COUNT)
    pos_rows = positions.reshape(3, summed_atom_energy)
    occ_rows = occupied.reshape(summed_atom_energy).astype(jnp.float32)
    safe_vector = jnp.array([CELL_SIDE, 0.0, 0.0], dtype=jnp.float32)

    def single_block_view(block_index):
        lattice_row = (block_index // blocks_per_row).astype(jnp.int32)
        first_col = (block_index % blocks_per_row * block_cells).astype(jnp.int32)
        zero_index = jnp.zeros((), jnp.int32)
        entry_codes = lax.dynamic_slice(neighbours, (lattice_row, first_col, zero_index, zero_index), (1, block_cells, CELL_ATOM_SLOTS, NEIGHBOUR_SLOTS))[0]
        cell_cols = first_col + jnp.arange(block_cells, dtype=jnp.int32)
        is_used = entry_codes < 9 * CELL_ATOM_SLOTS
        cell_code = entry_codes // CELL_ATOM_SLOTS
        horizontal_stride = jnp.where(is_used, cell_code // 3 - 1, 0).astype(jnp.int32)
        step_y = jnp.where(is_used, cell_code % 3 - 1, 0).astype(jnp.int32)
        slot_index = jnp.where(is_used, entry_codes % CELL_ATOM_SLOTS, 0).astype(jnp.int32)
        target_column = (lattice_row + horizontal_stride) % SLAB_CELL_COLUMNS
        target_y = (cell_cols[:, None, None] + step_y) % SLAB_CELL_ROWS
        target_rows = ((target_column * SLAB_CELL_ROWS + target_y) * CELL_ATOM_SLOTS + slot_index).astype(jnp.int32)
        own_rows = ((lattice_row * SLAB_CELL_ROWS + cell_cols)[:, None] * CELL_ATOM_SLOTS + jnp.arange(CELL_ATOM_SLOTS, dtype=jnp.int32)[None, :]).astype(jnp.int32)
        neigh_coords = jnp.moveaxis(pos_rows[:, target_rows], 0, -1)
        cell_steps = jnp.stack([horizontal_stride.astype(jnp.float32) * CELL_SIDE, step_y.astype(jnp.float32) * CELL_SIDE, jnp.zeros(horizontal_stride.shape, jnp.float32)], axis=-1)
        own_coords = jnp.moveaxis(pos_rows[:, own_rows], 0, -1)
        raw_vectors = neigh_coords + cell_steps - own_coords[:, :, None, :]
        vectors = jnp.where(is_used[..., None], raw_vectors, safe_vector)
        weights = is_used.astype(jnp.float32) * occ_rows[target_rows]
        atom_count = block_cells * CELL_ATOM_SLOTS
        energy_values, edge_gradient = block_step(feat_rows[target_rows].reshape(atom_count, NEIGHBOUR_SLOTS, 9, CHANNEL_COUNT), vectors.reshape(atom_count, NEIGHBOUR_SLOTS, 3), weights.reshape(atom_count, NEIGHBOUR_SLOTS), occ_rows[own_rows].reshape(atom_count), radial_weight, mix_weight, out_weight)
        return (energy_values, edge_gradient, target_rows.reshape(atom_count, NEIGHBOUR_SLOTS))
    energy_values, edge_gradient, target_sites = lax.map(single_block_view, jnp.arange(SLAB_CELL_COLUMNS * blocks_per_row, dtype=jnp.int32))
    edge_gradient = edge_gradient.reshape(summed_atom_energy, NEIGHBOUR_SLOTS, 3)
    self_force_term = lax.optimization_barrier(jnp.sum(edge_gradient, axis=1))
    neighbour_force_term = jnp.zeros((summed_atom_energy, 3), edge_gradient.dtype).at[target_sites.reshape(-1)].add(-edge_gradient.reshape(-1, 3))
    forces = jnp.transpose(self_force_term + neighbour_force_term).reshape(3, SLAB_CELL_COLUMNS, SLAB_CELL_ROWS, CELL_ATOM_SLOTS)
    slot_energy_values = energy_values.reshape(SLAB_CELL_COLUMNS, SLAB_CELL_ROWS, CELL_ATOM_SLOTS)
    return (forces, slot_energy_values, jnp.sum(slot_energy_values))
```

```python
import math

import jax
import jax.numpy as jnp
from jax import lax
from jax.experimental import pallas as pl
from jax.experimental.pallas import tpu as pltpu
from jax.sharding import Mesh, PartitionSpec as P

C = 128
NB = 8
GROUPS = 4
ROWS = 32
LEAD = (0, 3, 3, 3, 5, 5, 5, 5, 5)
PLAIN = (4, 4, 4, 6, 6, 6, 6, 6)
PAIRED = (1, 1, 1, 2, 2, 2, 2, 2)
R3 = math.sqrt(3.0)
R5 = math.sqrt(5.0)
R15 = math.sqrt(15.0)
F32 = jnp.float32
BF16 = jnp.bfloat16
NT = (((1,), (1,)), ((), ()))


def count_kernel(neighbours, counts):
    lanes = lax.broadcasted_iota(jnp.int32, (ROWS, C), 1)
    rows = lax.broadcasted_iota(jnp.int32, (ROWS, ROWS), 0)
    own_y = rows >> 4
    own_x = (rows >> 3) & 1
    for q in range(GROUPS):
        code = jnp.concatenate(
            [neighbours[x, 2 * q + y] for y in range(2) for x in range(2)], axis=0
        )
        cell = code >> 3
        step_x = (cell * 11) >> 5
        x = own_x + step_x
        y = own_y + cell - 3 * step_x
        column = jnp.where(x == 0, 2, jnp.where(x == 3, 3, x - 1))
        place = jnp.where(code < 72, (y * 4 + column) * 8 + (code & 7), -1)
        total = jnp.zeros((ROWS, C), F32)
        for k in range(32):
            total = total + jnp.where(lanes == place[:, k : k + 1], 1.0, 0.0)
        counts[q] = total


def weighted(products, weight, path):
    total = None
    for b in range(NB):
        term = weight[path, b : b + 1, :] * products[ROWS * b : ROWS * (b + 1)]
        total = term if total is None else total + term
    return total


def main_kernel(
    col_a, col_b, col_l, col_r, down, up, counts, weight, mix, out_weight,
    rows_out, near_out, send_down, send_up,
    table, geometry, edge, message, back, values, near,
):
    columns = (col_a, col_b, col_l, col_r)
    for m in range(10):
        for y in range(10):
            if y == 0:
                tiles = [down[i, m] for i in range(4)]
            elif y == 9:
                tiles = [up[i, m] for i in range(4)]
            else:
                tiles = [column[y - 1, m] for column in columns]
            rows = jnp.concatenate([tile.astype(F32) for tile in tiles], axis=0)
            table[32 * y : 32 * y + 32, C * m : C * m + C] = rows.astype(BF16)
    near[...] = jnp.zeros_like(near)

    piece = lax.broadcasted_iota(jnp.int32, (16, C), 1)
    which = lax.broadcasted_iota(jnp.int32, (16, C), 0) * 3
    pick_rows = jnp.where((piece >= which) & (piece < which + 3), 1.0, 0.0).astype(BF16)
    piece = lax.broadcasted_iota(jnp.int32, (C, 4 * C), 0)
    which = (lax.broadcasted_iota(jnp.int32, (C, 4 * C), 1) >> 7) * 3
    pick_columns = jnp.where((piece >= which) & (piece < which + 3), 1.0, 0.0).astype(BF16)
    lane = lax.broadcasted_iota(jnp.int32, (1, C), 1)
    column = (lane >> 3) & 3
    place_x = jnp.where(column == 2, 0, jnp.where(column == 3, 3, column + 1))
    shift_x = place_x.astype(F32) * 5.0
    shift_y = (lane >> 5).astype(F32) * 5.0
    row = lax.broadcasted_iota(jnp.int32, (ROWS, C), 0)
    own_shift_x = ((row >> 3) & 1).astype(F32) * 5.0 + 5.0
    own_shift_y = (row >> 4).astype(F32) * 5.0 + 5.0

    def block_of(q):
        return pl.ds(pl.multiple_of(q * 64, 64), C)

    def own_values(q):
        base = pl.multiple_of(q * 64, 64)
        own = jnp.concatenate(
            [
                table[pl.ds(base + 32, 16), 9 * C : 10 * C],
                table[pl.ds(base + 64, 16), 9 * C : 10 * C],
            ],
            axis=0,
        )
        return jnp.dot(own, pick_columns, preferred_element_type=F32)

    def forward(q, carry):
        block = block_of(q)
        around = lax.dot_general(
            pick_rows, table[block, 9 * C : 10 * C], NT, preferred_element_type=F32
        )
        own = own_values(q)
        rx = (around[0:1] + shift_x) - (own[:, 0:C] + own_shift_x)
        ry = (around[1:2] + shift_y) - (own[:, C : 2 * C] + own_shift_y)
        rz = around[2:3] - own[:, 2 * C : 3 * C]
        times = counts[q]
        dist_sq = rx * rx + ry * ry + rz * rz
        inside = (times > 0.5) & (dist_sq < 25.0)
        dist_sq = jnp.where(inside, dist_sq, 25.0)
        fall = jnp.where(inside, 1.0 - dist_sq * 0.04, 0.0)
        inv = lax.rsqrt(dist_sq)
        inv = inv * (1.5 - 0.5 * dist_sq * inv * inv)
        turn = dist_sq * inv * (math.pi / 5.0) - math.pi / 2.0
        sq = turn * turn
        cosine = jnp.full_like(sq, 1.0 / math.factorial(12))
        for order in (10, 8, 6, 4, 2, 0):
            sign = 1.0 if order % 4 == 0 else -1.0
            cosine = cosine * sq + sign / math.factorial(order)
        sine = jnp.full_like(sq, 1.0 / math.factorial(13))
        for order in (11, 9, 7, 5, 3, 1):
            sign = 1.0 if order % 4 == 1 else -1.0
            sine = sine * sq + sign / math.factorial(order)
        s_now, c_now = cosine, -sine * turn
        twice = 2.0 * c_now
        s_last, c_last = jnp.zeros_like(sq), jnp.ones_like(sq)
        amount = times * around[3:4]
        base = amount * fall * fall * inv
        slope = -(amount * fall) * (fall * inv * inv + 0.16)
        ux, uy, uz = rx * inv, ry * inv, rz * inv
        harmonics = (
            None,
            R3 * ux,
            R3 * uy,
            R3 * uz,
            R15 * ux * uy,
            R15 * uy * uz,
            (0.5 * R5) * (3.0 * uz * uz - 1.0),
            R15 * ux * uz,
            (0.5 * R15) * (ux * ux - uy * uy),
        )
        edge[q, 0] = inv
        for g in range(1, 9):
            edge[q, g] = harmonics[g]
        for b in range(NB):
            radial = s_now * base
            edge[q, 9 + b] = radial
            edge[q, 17 + b] = c_now * base * ((b + 1) * math.pi / 5.0) + s_now * slope
            spot = slice(ROWS * b, ROWS * b + ROWS)
            geometry[0, spot] = radial.astype(BF16)
            for g in range(1, 9):
                geometry[g, spot] = (radial * harmonics[g]).astype(BF16)
            s_now, s_last = twice * s_now - s_last, s_now
            c_now, c_last = twice * c_now - c_last, c_now
        messages = [None] * 9
        for m in (0, 2, 4, 6, 8):
            width = 1 if m == 8 else 2
            products = jnp.dot(
                geometry[0], table[block, C * m : C * (m + width)], preferred_element_type=F32
            )
            for j in range(width):
                path = 0 if m + j == 0 else PLAIN[m + j - 1]
                messages[m + j] = weighted(products[:, C * j : C * j + C], weight, path)
        first = table[block, 0:C]
        for g in range(1, 9):
            both = jnp.concatenate([first, table[block, C * g : C * g + C]], axis=1)
            products = jnp.dot(geometry[g], both, preferred_element_type=F32)
            messages[g] = messages[g] + weighted(products[:, :C], weight, LEAD[g])
            messages[0] = messages[0] + weighted(products[:, C:], weight, PAIRED[g - 1])
        for g in range(9):
            message[g] = messages[g].astype(BF16)
        mixed = jnp.dot(message[...].reshape(9 * ROWS, C), mix[...], preferred_element_type=F32)
        mixed = mixed.reshape(9, ROWS, C)
        z = mixed[0]
        for g in range(1, 9):
            z = z + mixed[g] * mixed[g]
        gate = 1.0 / (1.0 + jnp.exp(-z))
        scale = own[:, 3 * C : 4 * C] * out_weight[0:1]
        spot = pl.ds(pl.multiple_of(q * ROWS, ROWS), ROWS)
        values[3, spot] = scale * (z * gate)
        grad = scale * gate * (1.0 + z * (1.0 - gate))
        message[0] = grad.astype(BF16)
        grad = 2.0 * grad
        for g in range(1, 9):
            message[g] = (grad * mixed[g]).astype(BF16)
        returned = lax.dot_general(
            message[...].reshape(9 * ROWS, C), mix[...], NT, preferred_element_type=F32
        )
        back[...] = returned.reshape(9, ROWS, C)

        def spread(g, path):
            return jnp.concatenate(
                [(weight[path, b : b + 1, :] * back[g]).astype(BF16) for b in range(NB)], axis=0
            )

        wide = jnp.concatenate([spread(0, 0)] + [spread(g, PLAIN[g - 1]) for g in range(1, 9)], axis=1)
        grads = lax.dot_general(wide, table[block, 0 : 9 * C], NT, preferred_element_type=F32)
        along = [None] * NB
        sums = [None] * 9
        for b in range(NB):
            along[b] = grads[ROWS * b : ROWS * b + ROWS]
        paired = {1: spread(0, 1), 2: spread(0, 2)}
        for g in range(1, 9):
            both = jnp.concatenate([first, table[block, C * g : C * g + C]], axis=1)
            wide = jnp.concatenate([spread(g, LEAD[g]), paired[PAIRED[g - 1]]], axis=1)
            grads = lax.dot_general(wide, both, NT, preferred_element_type=F32)
            harmonic = edge[q, g]
            total = None
            for b in range(NB):
                part = grads[ROWS * b : ROWS * b + ROWS]
                along[b] = along[b] + part * harmonic
                term = part * edge[q, 9 + b]
                total = term if total is None else total + term
            sums[g] = total
        radial = None
        for b in range(NB):
            term = along[b] * edge[q, 17 + b]
            radial = term if radial is None else radial + term
        inv = edge[q, 0]
        ux, uy, uz = (edge[q, g] * (1.0 / R3) for g in (1, 2, 3))
        vx = R3 * sums[1] + R15 * (uy * sums[4] + uz * sums[7] + ux * sums[8])
        vy = R3 * sums[2] + R15 * (ux * sums[4] + uz * sums[5] - uy * sums[8])
        vz = R3 * sums[3] + R15 * (uy * sums[5] + ux * sums[7]) + (3.0 * R5) * uz * sums[6]
        inward = radial - inv * (ux * vx + uy * vy + uz * vz)
        for axis, (v, unit) in enumerate(((vx, ux), (vy, uy), (vz, uz))):
            gradient = inward * unit + inv * v
            values[axis, spot] = gradient
            near[axis, pl.ds(q, 1)] = jnp.sum(gradient, axis=0, keepdims=True)
        return carry

    lax.fori_loop(0, GROUPS, forward, 0)
    rows_out[...] = jnp.zeros_like(rows_out)
    send_down[...] = jnp.zeros_like(send_down)
    send_up[...] = jnp.zeros_like(send_up)
    for kind in range(4):
        rows_out[kind : kind + 1] = jnp.sum(values[kind].T, axis=0, keepdims=True)
    low = lax.broadcasted_iota(jnp.int32, (8, C), 1) < 64
    for axis in range(3):
        part = near[axis]
        later = pltpu.roll(pltpu.roll(part, 64, 1), 1, 0)
        pairs = jnp.where(low, part + later, 0.0)
        near_out[axis] = pairs
        send_down[axis : axis + 1] = pairs[0:1]
        send_up[axis : axis + 1] = pairs[4:5]


def main_call(*arrays):
    rows = jax.ShapeDtypeStruct((8, C), F32)
    return pl.pallas_call(
        main_kernel,
        out_shape=(rows, jax.ShapeDtypeStruct((3, 8, C), F32), rows, rows),
        in_specs=[pl.BlockSpec(memory_space=pltpu.VMEM)] * 10,
        out_specs=(pl.BlockSpec(memory_space=pltpu.VMEM),) * 4,
        scratch_shapes=[
            pltpu.VMEM((320, 10 * C), BF16),
            pltpu.VMEM((9, NB * ROWS, C), BF16),
            pltpu.VMEM((GROUPS, 25, ROWS, C), F32),
            pltpu.VMEM((9, ROWS, C), BF16),
            pltpu.VMEM((9, ROWS, C), F32),
            pltpu.VMEM((4, C, C), F32),
            pltpu.VMEM((3, 8, C), F32),
        ],
        compiler_params=pltpu.CompilerParams(vmem_limit_bytes=40 * 1024 * 1024),
        name="interact",
    )(*arrays)


def count_call(neighbours):
    return pl.pallas_call(
        count_kernel,
        out_shape=jax.ShapeDtypeStruct((GROUPS, ROWS, C), F32),
        in_specs=[pl.BlockSpec(memory_space=pltpu.VMEM)],
        out_specs=pl.BlockSpec(memory_space=pltpu.VMEM),
        compiler_params=pltpu.CompilerParams(vmem_limit_bytes=16 * 1024 * 1024),
        cost_estimate=pl.CostEstimate(flops=2_000_000, bytes_accessed=1_000_000, transcendentals=0),
        name="count",
    )(neighbours)


def ring(size, step):
    return [(i, (i + step) % size) for i in range(size)]


def packed_places(positions, occupied):
    pieces = []
    for axis in range(3):
        rest = positions[axis]
        for _ in range(3):
            piece = lax.reduce_precision(rest, 8, 7)
            pieces.append(piece)
            rest = rest - piece
    pieces.append(occupied.astype(F32))
    packed = jnp.stack(pieces, axis=-1)
    return jnp.pad(packed, ((0, 0), (0, 0), (0, 0), (0, C - 10))).astype(BF16)


def on_device(features, positions, occupied, neighbours, radial_weight, mix_weight, out_weight, *, outer, inner):
    gy = outer + inner
    size_x = lax.axis_size("gx")
    size_y = lax.axis_size(gy)
    counts = count_call(neighbours)
    own = jnp.concatenate(
        [jnp.transpose(features, (0, 1, 3, 2, 4)), packed_places(positions, occupied)[:, :, None]],
        axis=2,
    )
    col_a, col_b = own[0], own[1]
    col_l = lax.ppermute(col_b, "gx", ring(size_x, 1))
    col_r = lax.ppermute(col_a, "gx", ring(size_x, -1))
    columns = (col_a, col_b, col_l, col_r)
    down = lax.ppermute(jnp.stack([c[7] for c in columns]), gy, ring(size_y, 1))
    up = lax.ppermute(jnp.stack([c[0] for c in columns]), gy, ring(size_y, -1))
    rows, near, send_down, send_up = main_call(
        col_a, col_b, col_l, col_r, down, up, counts, radial_weight, mix_weight, out_weight[None]
    )
    from_up = lax.ppermute(send_down, gy, ring(size_y, -1))
    from_down = lax.ppermute(send_up, gy, ring(size_y, 1))
    energy = rows[3:4]
    plane = size_x * lax.axis_size(outer)
    gathered = lax.all_to_all(jnp.broadcast_to(energy[None], (plane, 1, C)), ("gx",) + outer, 0, 0)
    energy_plane = jnp.sum(gathered, axis=0)

    lane = jnp.arange(C)
    low = (lane < 32)[None, None, :]
    high = ((lane >= 32) & (lane < 64))[None, None, :]
    pair = jnp.arange(8)[None, :, None]
    near = near + jnp.where((pair == 0) & high, from_down[:3, None], 0.0)
    near = near + jnp.where((pair == 4) & low, from_up[:3, None], 0.0)
    from_left = lax.ppermute(near, "gx", ring(size_x, 1))
    from_right = lax.ppermute(near, "gx", ring(size_x, -1))
    depth = lax.axis_size(inner)
    gathered = lax.all_to_all(jnp.broadcast_to(energy_plane[None], (depth, 1, C)), inner, 0, 0)
    total_energy = jnp.sum(gathered)

    def cells(block):
        return block[:, :5, :64].reshape(3, 10, 4, 8)[:, 1:9]

    mine = cells(near)
    self_term = rows[:3].reshape(3, 8, 2, 8)
    first = self_term[:, :, 0] - mine[:, :, 0] - cells(from_left)[:, :, 3]
    second = self_term[:, :, 1] - mine[:, :, 1] - cells(from_right)[:, :, 2]
    forces = jnp.stack([first, second], axis=1)
    slot_energy_values = jnp.transpose(rows[3].reshape(8, 2, 8), (1, 0, 2))
    return forces, slot_energy_values, total_energy


def solution(mesh):
    size_x, size_y = mesh.shape["gx"], mesh.shape["gy"]
    depth = 16 if size_y % 16 == 0 else size_y // 2
    split = Mesh(mesh.devices.reshape(size_x, size_y // depth, depth), ("gx", "gya", "gyb"))
    outer, inner = ("gya",), ("gyb",)
    gy = outer + inner
    in_specs = (
        P("gx", gy, None, None, None),
        P(None, "gx", gy, None),
        P("gx", gy, None),
        P("gx", gy, None, None),
        P(),
        P(),
        P(),
    )
    out_specs = (P(None, "gx", gy, None), P("gx", gy, None), P())

    def program(*arrays):
        return on_device(*arrays, outer=outer, inner=inner)

    return jax.shard_map(
        program, mesh=split, in_specs=in_specs, out_specs=out_specs, check_vma=False
    )
```

```python
import math

import jax
import jax.numpy as jnp
from jax import lax
from jax.experimental import pallas as pl
from jax.experimental.pallas import tpu as pltpu
from jax.sharding import Mesh, PartitionSpec as P

C = 128
NB = 8
GROUPS = 4
ROWS = 32
LEAD = (0, 3, 3, 3, 5, 5, 5, 5, 5)
PLAIN = (4, 4, 4, 6, 6, 6, 6, 6)
PAIRED = (1, 1, 1, 2, 2, 2, 2, 2)
R3 = math.sqrt(3.0)
R5 = math.sqrt(5.0)
R15 = math.sqrt(15.0)
F32 = jnp.float32
BF16 = jnp.bfloat16
NT = (((1,), (1,)), ((), ()))


def pack_kernel(features, positions, occupied, neighbours, out):
    flat = [positions[axis, x] for axis in range(3) for x in range(2)]
    flat = flat + [occupied[x].astype(F32) for x in range(2)]
    flat = jnp.concatenate(flat, axis=0)
    flat = jnp.concatenate([flat, jnp.zeros((64, C - 8), F32)], axis=1)
    flat = jnp.concatenate([flat, jnp.zeros((64, C), F32)], axis=0).T[0:8]
    high = flat.astype(BF16).astype(F32)
    rest = flat - high
    middle = rest.astype(BF16).astype(F32)
    low = pltpu.roll((rest - middle), 2, 1)
    middle = pltpu.roll(middle, 1, 1)
    lane = lax.broadcasted_iota(jnp.int32, (8, C), 1)
    kind = jnp.where(lane < 64, lane & 15, 3)
    for x in range(2):
        for y in range(8):
            out[x, y, 0:9] = features[x, y]
            back = (C - (8 * x + y)) % C
            codes = jnp.concatenate(
                [jnp.zeros((8, 64), F32), neighbours[x, y].astype(F32), jnp.zeros((8, 32), F32)], axis=1
            )
            tile = jnp.where(kind == 2, pltpu.roll(low, back, 1), codes)
            tile = jnp.where(kind == 1, pltpu.roll(middle, back, 1), tile)
            tile = jnp.where(kind == 0, pltpu.roll(high, back, 1), tile)
            out[x, y, 9] = tile.astype(BF16)


def count(codes):
    lanes = lax.broadcasted_iota(jnp.int32, (ROWS, C), 1).astype(F32)
    rows = lax.broadcasted_iota(jnp.int32, (ROWS, C), 0)
    code = codes.astype(jnp.int32)
    cell = code >> 3
    step_x = (cell * 11) >> 5
    x = ((rows >> 3) & 1) + step_x
    y = (rows >> 4) + cell - 3 * step_x
    column = jnp.where(x == 0, 2, jnp.where(x == 3, 3, x - 1))
    place = jnp.where(code < 72, (y * 4 + column) * 8 + (code & 7), -1).astype(F32)
    total = jnp.zeros((ROWS, C), F32)
    for k in range(32):
        total = total + jnp.where(lanes == place[:, 64 + k : 65 + k], 1.0, 0.0)
    return total


def block_of(q):
    return pl.ds(pl.multiple_of(q * 64, 64), C)


def weighted(products, weight, path):
    total = None
    for b in range(NB):
        term = weight[path, b : b + 1, :] * products[ROWS * b : ROWS * (b + 1)]
        total = term if total is None else total + term
    return total


def forward_kernel(
    own, right, up, weight, mix, out_weight,
    energy_out, energies, table, edge, back,
    geometry, message,
):
    for m in range(10):
        for y in range(10):
            if y < 8:
                tiles = [own[1, y, m], right[0, y, m], own[0, y, m], right[1, y, m]]
            else:
                tiles = [up[i, y - 8, m] for i in (1, 2, 0, 3)]
            rows = jnp.concatenate([tile.astype(F32) for tile in tiles], axis=0)
            table[32 * y : 32 * y + 32, C * m : C * m + C] = rows.astype(BF16)

    piece = lax.broadcasted_iota(jnp.int32, (16, C), 1)
    which = lax.broadcasted_iota(jnp.int32, (16, C), 0) * 16
    pick_rows = jnp.where((which < 64) & (piece >= which) & (piece < which + 3), 1.0, 0.0).astype(BF16)
    piece = lax.broadcasted_iota(jnp.int32, (C, 4 * C), 0)
    which = (lax.broadcasted_iota(jnp.int32, (C, 4 * C), 1) >> 7) * 16
    pick_columns = jnp.where((piece >= which) & (piece < which + 3), 1.0, 0.0).astype(BF16)
    lane = lax.broadcasted_iota(jnp.int32, (1, C), 1)
    column = (lane >> 3) & 3
    place_x = jnp.where(column == 2, 0, jnp.where(column == 3, 3, column + 1))
    shift_x = place_x.astype(F32) * 5.0
    shift_y = (lane >> 5).astype(F32) * 5.0
    row = lax.broadcasted_iota(jnp.int32, (ROWS, C), 0)
    own_shift_x = ((row >> 3) & 1).astype(F32) * 5.0 + 5.0
    own_shift_y = (row >> 4).astype(F32) * 5.0 + 5.0

    def group_values(q):
        base = pl.multiple_of(q * 64, 64)
        return jnp.concatenate(
            [
                table[pl.ds(base + 32, 16), 9 * C : 10 * C],
                table[pl.ds(base + 64, 16), 9 * C : 10 * C],
            ],
            axis=0,
        )

    def forward(q, carry):
        block = block_of(q)
        around = lax.dot_general(
            pick_rows, table[block, 9 * C : 10 * C], NT, preferred_element_type=F32
        )
        mine = group_values(q)
        own_at = jnp.dot(mine, pick_columns, preferred_element_type=F32)
        rx = (around[0:1] + shift_x) - (own_at[:, 0:C] + own_shift_x)
        ry = (around[1:2] + shift_y) - (own_at[:, C : 2 * C] + own_shift_y)
        rz = around[2:3] - own_at[:, 2 * C : 3 * C]
        times = count(mine.astype(F32))
        dist_sq = rx * rx + ry * ry + rz * rz
        inside = (times > 0.5) & (dist_sq < 25.0)
        dist_sq = jnp.where(inside, dist_sq, 25.0)
        fall = jnp.where(inside, 1.0 - dist_sq * 0.04, 0.0)
        inv = lax.rsqrt(dist_sq)
        inv = inv * (1.5 - 0.5 * dist_sq * inv * inv)
        turn = dist_sq * inv * (math.pi / 5.0) - math.pi / 2.0
        sq = turn * turn
        cosine = jnp.full_like(sq, 1.0 / math.factorial(12))
        for order in (10, 8, 6, 4, 2, 0):
            sign = 1.0 if order % 4 == 0 else -1.0
            cosine = cosine * sq + sign / math.factorial(order)
        sine = jnp.full_like(sq, 1.0 / math.factorial(13))
        for order in (11, 9, 7, 5, 3, 1):
            sign = 1.0 if order % 4 == 1 else -1.0
            sine = sine * sq + sign / math.factorial(order)
        s_now, c_now = cosine, -sine * turn
        twice = 2.0 * c_now
        s_last, c_last = jnp.zeros_like(sq), jnp.ones_like(sq)
        amount = times * around[3:4]
        base = amount * fall * fall * inv
        slope = -(amount * fall) * (fall * inv * inv + 0.16)
        ux, uy, uz = rx * inv, ry * inv, rz * inv
        harmonics = (
            None,
            R3 * ux,
            R3 * uy,
            R3 * uz,
            R15 * ux * uy,
            R15 * uy * uz,
            (0.5 * R5) * (3.0 * uz * uz - 1.0),
            R15 * ux * uz,
            (0.5 * R15) * (ux * ux - uy * uy),
        )
        edge[q, 0] = inv
        for g in range(1, 9):
            edge[q, g] = harmonics[g]
        for b in range(NB):
            radial = s_now * base
            edge[q, 9 + b] = radial
            edge[q, 17 + b] = c_now * base * ((b + 1) * math.pi / 5.0) + s_now * slope
            spot = slice(ROWS * b, ROWS * b + ROWS)
            geometry[0, spot] = radial.astype(BF16)
            for g in range(1, 9):
                geometry[g, spot] = (radial * harmonics[g]).astype(BF16)
            s_now, s_last = twice * s_now - s_last, s_now
            c_now, c_last = twice * c_now - c_last, c_now
        messages = [None] * 9
        for m in (0, 2, 4, 6, 8):
            width = 1 if m == 8 else 2
            products = jnp.dot(
                geometry[0], table[block, C * m : C * (m + width)], preferred_element_type=F32
            )
            for j in range(width):
                path = 0 if m + j == 0 else PLAIN[m + j - 1]
                messages[m + j] = weighted(products[:, C * j : C * j + C], weight, path)
        first = table[block, 0:C]
        for g in range(1, 9):
            both = jnp.concatenate([first, table[block, C * g : C * g + C]], axis=1)
            products = jnp.dot(geometry[g], both, preferred_element_type=F32)
            messages[g] = messages[g] + weighted(products[:, :C], weight, LEAD[g])
            messages[0] = messages[0] + weighted(products[:, C:], weight, PAIRED[g - 1])
        for g in range(9):
            message[g] = messages[g].astype(BF16)
        mixed = jnp.dot(message[...].reshape(9 * ROWS, C), mix[...], preferred_element_type=F32)
        mixed = mixed.reshape(9, ROWS, C)
        z = mixed[0]
        for g in range(1, 9):
            z = z + mixed[g] * mixed[g]
        gate = 1.0 / (1.0 + jnp.exp(-z))
        scale = own_at[:, 3 * C : 4 * C] * out_weight[0:1]
        spot = pl.ds(pl.multiple_of(q * ROWS, ROWS), ROWS)
        energies[spot] = scale * (z * gate)
        grad = scale * gate * (1.0 + z * (1.0 - gate))
        message[0] = grad.astype(BF16)
        grad = 2.0 * grad
        for g in range(1, 9):
            message[g] = (grad * mixed[g]).astype(BF16)
        returned = lax.dot_general(
            message[...].reshape(9 * ROWS, C), mix[...], NT, preferred_element_type=F32
        )
        back[q] = returned.reshape(9, ROWS, C)
        return carry

    lax.fori_loop(0, GROUPS, forward, 0)
    energy_out[...] = jnp.zeros_like(energy_out)
    energy_out[0:1] = jnp.sum(energies[...].T, axis=0, keepdims=True)


def backward_kernel(table, edge, back, weight, energy, near_out, send_up, values, near):
    near[...] = jnp.zeros_like(near)

    def backward(q, carry):
        block = block_of(q)
        first = table[block, 0:C]
        spot = pl.ds(pl.multiple_of(q * ROWS, ROWS), ROWS)

        def spread(g, path):
            return jnp.concatenate(
                [(weight[path, b : b + 1, :] * back[q, g]).astype(BF16) for b in range(NB)], axis=0
            )

        wide = jnp.concatenate([spread(0, 0)] + [spread(g, PLAIN[g - 1]) for g in range(1, 9)], axis=1)
        grads = lax.dot_general(wide, table[block, 0 : 9 * C], NT, preferred_element_type=F32)
        along = [None] * NB
        sums = [None] * 9
        for b in range(NB):
            along[b] = grads[ROWS * b : ROWS * b + ROWS]
        paired = {1: spread(0, 1), 2: spread(0, 2)}
        for g in range(1, 9):
            both = jnp.concatenate([first, table[block, C * g : C * g + C]], axis=1)
            wide = jnp.concatenate([spread(g, LEAD[g]), paired[PAIRED[g - 1]]], axis=1)
            grads = lax.dot_general(wide, both, NT, preferred_element_type=F32)
            harmonic = edge[q, g]
            total = None
            for b in range(NB):
                part = grads[ROWS * b : ROWS * b + ROWS]
                along[b] = along[b] + part * harmonic
                term = part * edge[q, 9 + b]
                total = term if total is None else total + term
            sums[g] = total
        radial = None
        for b in range(NB):
            term = along[b] * edge[q, 17 + b]
            radial = term if radial is None else radial + term
        inv = edge[q, 0]
        ux, uy, uz = (edge[q, g] * (1.0 / R3) for g in (1, 2, 3))
        vx = R3 * sums[1] + R15 * (uy * sums[4] + uz * sums[7] + ux * sums[8])
        vy = R3 * sums[2] + R15 * (ux * sums[4] + uz * sums[5] - uy * sums[8])
        vz = R3 * sums[3] + R15 * (uy * sums[5] + ux * sums[7]) + (3.0 * R5) * uz * sums[6]
        inward = radial - inv * (ux * vx + uy * vy + uz * vz)
        for axis, (v, unit) in enumerate(((vx, ux), (vy, uy), (vz, uz))):
            gradient = inward * unit + inv * v
            values[axis, spot] = gradient
            near[axis, pl.ds(q, 1)] = jnp.sum(gradient, axis=0, keepdims=True)
        return carry

    lax.fori_loop(0, GROUPS, backward, 0)
    send_up[...] = jnp.zeros_like(send_up)
    near_out[...] = jnp.zeros_like(near_out)
    lane = lax.broadcasted_iota(jnp.int32, (8, C), 1)
    for kind in range(4):
        if kind < 3:
            part = near[kind]
            later = pltpu.roll(pltpu.roll(part, 64, 1), 1, 0)
            pairs = -(part + later)
            own = jnp.sum(values[kind].T, axis=0, keepdims=True)
        else:
            pairs = jnp.zeros((8, C), F32)
            own = energy[0:1]
        own = jnp.concatenate(
            [own] + [pltpu.roll(own, C - 32 * q, 1) for q in range(1, 4)] + [jnp.zeros((4, C), F32)], axis=0
        )
        pairs = pairs + jnp.where((lane >= 32) & (lane < 48), pltpu.roll(own, 32, 1), 0.0)
        own = pltpu.roll(pltpu.roll(own, C - 16, 1), 1, 0)
        pairs = jnp.where(lane < 64, pairs + jnp.where(lane < 16, own, 0.0), 0.0)
        near_out[kind] = pairs
        send_up[kind : kind + 1] = pairs[4:5]


VMEM = pl.BlockSpec(memory_space=pltpu.VMEM)


def pack_call(features, positions, occupied, neighbours):
    return pl.pallas_call(
        pack_kernel,
        out_shape=jax.ShapeDtypeStruct((2, 8, 10, 8, C), BF16),
        in_specs=[VMEM] * 4,
        out_specs=VMEM,
        compiler_params=pltpu.CompilerParams(vmem_limit_bytes=8 * 1024 * 1024),
        name="pack",
    )(features, positions, occupied, neighbours)


def forward_call(*arrays):
    return pl.pallas_call(
        forward_kernel,
        out_shape=(
            jax.ShapeDtypeStruct((8, C), F32),
            jax.ShapeDtypeStruct((C, C), F32),
            jax.ShapeDtypeStruct((320, 10 * C), BF16),
            jax.ShapeDtypeStruct((GROUPS, 25, ROWS, C), F32),
            jax.ShapeDtypeStruct((GROUPS, 9, ROWS, C), F32),
        ),
        in_specs=[VMEM] * 6,
        out_specs=(VMEM,) * 5,
        scratch_shapes=[
            pltpu.VMEM((9, NB * ROWS, C), BF16),
            pltpu.VMEM((9, ROWS, C), BF16),
        ],
        compiler_params=pltpu.CompilerParams(vmem_limit_bytes=20 * 1024 * 1024),
        cost_estimate=pl.CostEstimate(flops=4_000_000_000, bytes_accessed=8_000_000, transcendentals=0),
        name="forward",
    )(*arrays)


def backward_call(*arrays):
    return pl.pallas_call(
        backward_kernel,
        out_shape=(jax.ShapeDtypeStruct((4, 8, C), F32), jax.ShapeDtypeStruct((8, C), F32)),
        in_specs=[VMEM] * 5,
        out_specs=(VMEM,) * 2,
        scratch_shapes=[pltpu.VMEM((3, C, C), F32), pltpu.VMEM((3, 8, C), F32)],
        compiler_params=pltpu.CompilerParams(vmem_limit_bytes=20 * 1024 * 1024),
        cost_estimate=pl.CostEstimate(flops=4_000_000_000, bytes_accessed=8_000_000, transcendentals=0),
        name="backward",
    )(*arrays)


def ring(size, step):
    return [(i, (i + step) % size) for i in range(size)]


def on_device(features, positions, occupied, neighbours, radial_weight, mix_weight, out_weight, *, outer, inner):
    gy = outer + inner
    size_x = lax.axis_size("gx")
    size_y = lax.axis_size(gy)
    own = pack_call(jnp.transpose(features, (0, 1, 3, 2, 4)), positions, occupied, neighbours)
    right = lax.ppermute(own, "gx", ring(size_x, -1))
    up = lax.ppermute(jnp.concatenate([own[:, :2], right[:, :2]], axis=0), gy, ring(size_y, -1))
    energy, _, table, edge, back = forward_call(
        own, right, up, radial_weight, mix_weight, out_weight[None]
    )
    plane = size_x * lax.axis_size(outer)
    gathered = lax.all_to_all(
        jnp.broadcast_to(energy[None, :1], (plane, 1, C)), ("gx",) + outer, 0, 0
    )
    near, send_up = backward_call(table, edge, back, radial_weight, energy)
    energy_plane = jnp.sum(gathered, axis=0)
    depth = lax.axis_size(inner)
    gathered = lax.all_to_all(jnp.broadcast_to(energy_plane[None], (depth, 1, C)), inner, 0, 0)
    from_down = lax.ppermute(send_up, gy, ring(size_y, 1))
    near = near.at[:, 0].add(from_down[:4])[:, :4]
    from_left = lax.ppermute(near, "gx", ring(size_x, 1))
    total_energy = jnp.sum(gathered)

    def column(block, place):
        return block[:, :, :64].reshape(4, 8, 4, 8)[:, :, place]

    first = column(near, 2) + column(from_left, 1)
    second = column(near, 0) + column(from_left, 3)
    cells = jnp.stack([first, second], axis=1)
    return cells[:3], cells[3], total_energy


def solution(mesh):
    size_x, size_y = mesh.shape["gx"], mesh.shape["gy"]
    depth = 16 if size_y % 16 == 0 else size_y // 2
    split = Mesh(mesh.devices.reshape(size_x, size_y // depth, depth), ("gx", "gya", "gyb"))
    outer, inner = ("gya",), ("gyb",)
    gy = outer + inner
    in_specs = (
        P("gx", gy, None, None, None),
        P(None, "gx", gy, None),
        P("gx", gy, None),
        P("gx", gy, None, None),
        P(),
        P(),
        P(),
    )
    out_specs = (P(None, "gx", gy, None), P("gx", gy, None), P())

    def program(*arrays):
        return on_device(*arrays, outer=outer, inner=inner)

    return jax.shard_map(
        program, mesh=split, in_specs=in_specs, out_specs=out_specs, check_vma=False
    )
```

```python
import math

import jax
import jax.numpy as jnp
from jax import lax
from jax.experimental import pallas as pl
from jax.experimental.pallas import tpu as pltpu
from jax.sharding import Mesh, PartitionSpec as P

C = 128
NB = 8
GROUPS = 4
ROWS = 32
LEAD = (0, 3, 3, 3, 5, 5, 5, 5, 5)
PLAIN = (4, 4, 4, 6, 6, 6, 6, 6)
PAIRED = (1, 1, 1, 2, 2, 2, 2, 2)
R3 = math.sqrt(3.0)
R5 = math.sqrt(5.0)
R15 = math.sqrt(15.0)
F32 = jnp.float32
BF16 = jnp.bfloat16
NT = (((1,), (1,)), ((), ()))


def pack_kernel(features, places, present, lists, out, positions, occupied, neighbours, done):
    moves = [
        pltpu.make_async_copy(source, target, done.at[i])
        for i, (source, target) in enumerate(
            (
                (places, positions),
                (present, occupied),
                (lists, neighbours),
                (features, out.at[:, :, 0:9]),
            )
        )
    ]
    for move in moves:
        move.start()
    for move in moves[:3]:
        move.wait()
    flat = [positions[axis, x] for axis in range(3) for x in range(2)]
    flat = flat + [occupied[x].astype(F32) for x in range(2)]
    flat = jnp.concatenate(flat, axis=0)
    flat = jnp.concatenate([flat, jnp.zeros((64, C - 8), F32)], axis=1)
    flat = jnp.concatenate([flat, jnp.zeros((64, C), F32)], axis=0).T[0:8]
    high = flat.astype(BF16).astype(F32)
    rest = flat - high
    middle = rest.astype(BF16).astype(F32)
    low = pltpu.roll((rest - middle), 2, 1)
    middle = pltpu.roll(middle, 1, 1)
    lane = lax.broadcasted_iota(jnp.int32, (8, C), 1)
    kind = jnp.where(lane < 64, lane & 15, 3)
    for x in range(2):
        for y in range(8):
            back = (C - (8 * x + y)) % C
            codes = jnp.concatenate(
                [jnp.zeros((8, 64), F32), neighbours[x, y].astype(F32), jnp.zeros((8, 32), F32)], axis=1
            )
            tile = jnp.where(kind == 2, pltpu.roll(low, back, 1), codes)
            tile = jnp.where(kind == 1, pltpu.roll(middle, back, 1), tile)
            tile = jnp.where(kind == 0, pltpu.roll(high, back, 1), tile)
            out[x, y, 9] = tile.astype(BF16)
    moves[3].wait()


def count(codes):
    lanes = lax.broadcasted_iota(jnp.int32, (ROWS, C), 1).astype(F32)
    rows = lax.broadcasted_iota(jnp.int32, (ROWS, C), 0)
    code = codes.astype(jnp.int32)
    cell = code >> 3
    step_x = (cell * 11) >> 5
    x = ((rows >> 3) & 1) + step_x
    y = (rows >> 4) + cell - 3 * step_x
    column = jnp.where(x == 0, 2, jnp.where(x == 3, 3, x - 1))
    place = jnp.where(code < 72, (y * 4 + column) * 8 + (code & 7), -1).astype(F32)
    total = jnp.zeros((ROWS, C), F32)
    for k in range(32):
        total = total + jnp.where(lanes == place[:, 64 + k : 65 + k], 1.0, 0.0)
    return total


def block_of(q):
    return pl.ds(pl.multiple_of(q * 64, 64), C)


def weighted(products, weight, path):
    total = None
    for b in range(NB):
        term = weight[path, b : b + 1, :] * products[ROWS * b : ROWS * (b + 1)]
        total = term if total is None else total + term
    return total


def group_forward(table, weight, mix, out_weight, edge, back, energies, geometry, message):
    piece = lax.broadcasted_iota(jnp.int32, (16, C), 1)
    which = lax.broadcasted_iota(jnp.int32, (16, C), 0) * 16
    pick_rows = jnp.where((which < 64) & (piece >= which) & (piece < which + 3), 1.0, 0.0).astype(BF16)
    piece = lax.broadcasted_iota(jnp.int32, (C, 4 * C), 0)
    which = (lax.broadcasted_iota(jnp.int32, (C, 4 * C), 1) >> 7) * 16
    pick_columns = jnp.where((piece >= which) & (piece < which + 3), 1.0, 0.0).astype(BF16)
    lane = lax.broadcasted_iota(jnp.int32, (1, C), 1)
    column = (lane >> 3) & 3
    place_x = jnp.where(column == 2, 0, jnp.where(column == 3, 3, column + 1))
    shift_x = place_x.astype(F32) * 5.0
    shift_y = (lane >> 5).astype(F32) * 5.0
    row = lax.broadcasted_iota(jnp.int32, (ROWS, C), 0)
    own_shift_x = ((row >> 3) & 1).astype(F32) * 5.0 + 5.0
    own_shift_y = (row >> 4).astype(F32) * 5.0 + 5.0

    def group_values(q):
        base = pl.multiple_of(q * 64, 64)
        return jnp.concatenate(
            [
                table[pl.ds(base + 32, 16), 9 * C : 10 * C],
                table[pl.ds(base + 64, 16), 9 * C : 10 * C],
            ],
            axis=0,
        )

    def forward(q, carry):
        block = block_of(q)
        around = lax.dot_general(
            pick_rows, table[block, 9 * C : 10 * C], NT, preferred_element_type=F32
        )
        mine = group_values(q)
        own_at = jnp.dot(mine, pick_columns, preferred_element_type=F32)
        rx = (around[0:1] + shift_x) - (own_at[:, 0:C] + own_shift_x)
        ry = (around[1:2] + shift_y) - (own_at[:, C : 2 * C] + own_shift_y)
        rz = around[2:3] - own_at[:, 2 * C : 3 * C]
        times = count(mine.astype(F32))
        dist_sq = rx * rx + ry * ry + rz * rz
        inside = (times > 0.5) & (dist_sq < 25.0)
        dist_sq = jnp.where(inside, dist_sq, 25.0)
        fall = jnp.where(inside, 1.0 - dist_sq * 0.04, 0.0)
        inv = lax.rsqrt(dist_sq)
        inv = inv * (1.5 - 0.5 * dist_sq * inv * inv)
        turn = dist_sq * inv * (math.pi / 5.0) - math.pi / 2.0
        sq = turn * turn
        cosine = jnp.full_like(sq, 1.0 / math.factorial(12))
        for order in (10, 8, 6, 4, 2, 0):
            sign = 1.0 if order % 4 == 0 else -1.0
            cosine = cosine * sq + sign / math.factorial(order)
        sine = jnp.full_like(sq, 1.0 / math.factorial(13))
        for order in (11, 9, 7, 5, 3, 1):
            sign = 1.0 if order % 4 == 1 else -1.0
            sine = sine * sq + sign / math.factorial(order)
        s_now, c_now = cosine, -sine * turn
        twice = 2.0 * c_now
        s_last, c_last = jnp.zeros_like(sq), jnp.ones_like(sq)
        amount = times * around[3:4]
        base = amount * fall * fall * inv
        slope = -(amount * fall) * (fall * inv * inv + 0.16)
        ux, uy, uz = rx * inv, ry * inv, rz * inv
        harmonics = (
            None,
            R3 * ux,
            R3 * uy,
            R3 * uz,
            R15 * ux * uy,
            R15 * uy * uz,
            (0.5 * R5) * (3.0 * uz * uz - 1.0),
            R15 * ux * uz,
            (0.5 * R15) * (ux * ux - uy * uy),
        )
        edge[q, 0] = inv
        for g in range(1, 9):
            edge[q, g] = harmonics[g]
        for b in range(NB):
            radial = s_now * base
            edge[q, 9 + b] = radial
            edge[q, 17 + b] = c_now * base * ((b + 1) * math.pi / 5.0) + s_now * slope
            spot = slice(ROWS * b, ROWS * b + ROWS)
            geometry[0, spot] = radial.astype(BF16)
            for g in range(1, 9):
                geometry[g, spot] = (radial * harmonics[g]).astype(BF16)
            s_now, s_last = twice * s_now - s_last, s_now
            c_now, c_last = twice * c_now - c_last, c_now
        messages = [None] * 9
        for m in (0, 2, 4, 6, 8):
            width = 1 if m == 8 else 2
            products = jnp.dot(
                geometry[0], table[block, C * m : C * (m + width)], preferred_element_type=F32
            )
            for j in range(width):
                path = 0 if m + j == 0 else PLAIN[m + j - 1]
                messages[m + j] = weighted(products[:, C * j : C * j + C], weight, path)
        first = table[block, 0:C]
        for g in range(1, 9):
            both = jnp.concatenate([first, table[block, C * g : C * g + C]], axis=1)
            products = jnp.dot(geometry[g], both, preferred_element_type=F32)
            messages[g] = messages[g] + weighted(products[:, :C], weight, LEAD[g])
            messages[0] = messages[0] + weighted(products[:, C:], weight, PAIRED[g - 1])
        for g in range(9):
            message[g] = messages[g].astype(BF16)
        mixed = jnp.dot(message[...].reshape(9 * ROWS, C), mix[...], preferred_element_type=F32)
        mixed = mixed.reshape(9, ROWS, C)
        z = mixed[0]
        for g in range(1, 9):
            z = z + mixed[g] * mixed[g]
        gate = 1.0 / (1.0 + jnp.exp(-z))
        scale = own_at[:, 3 * C : 4 * C] * out_weight[0:1]
        spot = pl.ds(pl.multiple_of(q * ROWS, ROWS), ROWS)
        energies[spot] = scale * (z * gate)
        grad = scale * gate * (1.0 + z * (1.0 - gate))
        message[0] = grad.astype(BF16)
        grad = 2.0 * grad
        for g in range(1, 9):
            message[g] = (grad * mixed[g]).astype(BF16)
        returned = lax.dot_general(
            message[...].reshape(9 * ROWS, C), mix[...], NT, preferred_element_type=F32
        )
        back[q] = returned.reshape(9, ROWS, C)
        return carry

    return forward


def fill(table, row, m, tiles):
    rows = jnp.concatenate([tile.astype(F32) for tile in tiles], axis=0)
    table[32 * row : 32 * row + 32, C * m : C * m + C] = rows.astype(BF16)


def early_kernel(own, right, weight, mix, out_weight, energies, table, edge, back, geometry, message):
    for m in range(10):
        for y in range(8):
            fill(table, y, m, [own[1, y, m], right[0, y, m], own[0, y, m], right[1, y, m]])
    step = group_forward(table, weight, mix, out_weight, edge, back, energies, geometry, message)
    lax.fori_loop(0, GROUPS - 1, step, 0)


def late_kernel(
    known, up, early, weight, mix, out_weight,
    energy_out, spread_out, table, edge, back,
    energies, geometry, message,
):
    table[0:64] = known[192:256]
    for m in range(10):
        for y in range(2):
            fill(table, 2 + y, m, [up[i, y, m] for i in (1, 2, 0, 3)])
    group_forward(table, weight, mix, out_weight, edge, back, energies, geometry, message)(0, 0)
    total = jnp.concatenate([early[...], energies[...]], axis=0)
    total = jnp.sum(total.T, axis=0, keepdims=True)
    energy_out[...] = jnp.broadcast_to(total, energy_out.shape)
    spread_out[...] = jnp.broadcast_to(total[None], spread_out.shape)


def relay_kernel(gathered, out):
    total = jnp.sum(gathered[...], axis=0, keepdims=True)
    out[...] = jnp.broadcast_to(total, out.shape)


def group_backward(table, edge, back, weight, values, near, ahead):
    def backward(q, carry):
        block = block_of(q)
        first = table[block, 0:C]
        spot = pl.ds(pl.multiple_of((q + ahead) * ROWS, ROWS), ROWS)

        def spread(g, path):
            return jnp.concatenate(
                [(weight[path, b : b + 1, :] * back[q, g]).astype(BF16) for b in range(NB)], axis=0
            )

        wide = jnp.concatenate([spread(0, 0)] + [spread(g, PLAIN[g - 1]) for g in range(1, 9)], axis=1)
        grads = lax.dot_general(wide, table[block, 0 : 9 * C], NT, preferred_element_type=F32)
        along = [None] * NB
        sums = [None] * 9
        for b in range(NB):
            along[b] = grads[ROWS * b : ROWS * b + ROWS]
        paired = {1: spread(0, 1), 2: spread(0, 2)}
        for g in range(1, 9):
            both = jnp.concatenate([first, table[block, C * g : C * g + C]], axis=1)
            wide = jnp.concatenate([spread(g, LEAD[g]), paired[PAIRED[g - 1]]], axis=1)
            grads = lax.dot_general(wide, both, NT, preferred_element_type=F32)
            harmonic = edge[q, g]
            total = None
            for b in range(NB):
                part = grads[ROWS * b : ROWS * b + ROWS]
                along[b] = along[b] + part * harmonic
                term = part * edge[q, 9 + b]
                total = term if total is None else total + term
            sums[g] = total
        radial = None
        for b in range(NB):
            term = along[b] * edge[q, 17 + b]
            radial = term if radial is None else radial + term
        inv = edge[q, 0]
        ux, uy, uz = (edge[q, g] * (1.0 / R3) for g in (1, 2, 3))
        vx = R3 * sums[1] + R15 * (uy * sums[4] + uz * sums[7] + ux * sums[8])
        vy = R3 * sums[2] + R15 * (ux * sums[4] + uz * sums[5] - uy * sums[8])
        vz = R3 * sums[3] + R15 * (uy * sums[5] + ux * sums[7]) + (3.0 * R5) * uz * sums[6]
        inward = radial - inv * (ux * vx + uy * vy + uz * vz)
        for axis, (v, unit) in enumerate(((vx, ux), (vy, uy), (vz, uz))):
            gradient = inward * unit + inv * v
            values[axis, spot] = gradient
            near[axis, pl.ds(q + ahead, 1)] = jnp.sum(gradient, axis=0, keepdims=True)
        return carry

    return backward


def backward_kernel(
    table, edge, back, late_table, late_edge, late_back, weight, energy,
    near_out, send_up, values, near,
):
    near[...] = jnp.zeros_like(near)
    lax.fori_loop(0, GROUPS - 1, group_backward(table, edge, back, weight, values, near, 0), 0)
    group_backward(late_table, late_edge, late_back, weight, values, near, GROUPS - 1)(0, 0)
    send_up[...] = jnp.zeros_like(send_up)
    near_out[...] = jnp.zeros_like(near_out)
    lane = lax.broadcasted_iota(jnp.int32, (8, C), 1)
    for kind in range(4):
        if kind < 3:
            part = near[kind]
            later = pltpu.roll(pltpu.roll(part, 64, 1), 1, 0)
            pairs = -(part + later)
            own = jnp.sum(values[kind].T, axis=0, keepdims=True)
        else:
            pairs = jnp.zeros((8, C), F32)
            own = energy[0:1]
        own = jnp.concatenate(
            [own] + [pltpu.roll(own, C - 32 * q, 1) for q in range(1, 4)] + [jnp.zeros((4, C), F32)], axis=0
        )
        pairs = pairs + jnp.where((lane >= 32) & (lane < 48), pltpu.roll(own, 32, 1), 0.0)
        own = pltpu.roll(pltpu.roll(own, C - 16, 1), 1, 0)
        pairs = jnp.where(lane < 64, pairs + jnp.where(lane < 16, own, 0.0), 0.0)
        near_out[kind] = pairs
        send_up[kind : kind + 1] = pairs[4:5]


VMEM = pl.BlockSpec(memory_space=pltpu.VMEM)


def pack_call(features, positions, occupied, neighbours):
    return pl.pallas_call(
        pack_kernel,
        out_shape=jax.ShapeDtypeStruct((2, 8, 10, 8, C), BF16),
        in_specs=[pl.BlockSpec(memory_space=pl.ANY)] * 4,
        out_specs=VMEM,
        scratch_shapes=[
            pltpu.VMEM(positions.shape, F32),
            pltpu.VMEM(occupied.shape, jnp.int32),
            pltpu.VMEM(neighbours.shape, jnp.int32),
            pltpu.SemaphoreType.DMA((4,)),
        ],
        name="pack",
    )(features, positions, occupied, neighbours)


def results(groups, rows):
    return (
        jax.ShapeDtypeStruct((rows, 10 * C), BF16),
        jax.ShapeDtypeStruct((groups, 25, ROWS, C), F32),
        jax.ShapeDtypeStruct((groups, 9, ROWS, C), F32),
    )


SCRATCH = [pltpu.VMEM((9, NB * ROWS, C), BF16), pltpu.VMEM((9, ROWS, C), BF16)]


def early_call(*arrays):
    return pl.pallas_call(
        early_kernel,
        out_shape=(jax.ShapeDtypeStruct((3 * ROWS, C), F32),) + results(3, 256),
        in_specs=[VMEM] * 5,
        out_specs=(VMEM,) * 4,
        scratch_shapes=SCRATCH,
        compiler_params=pltpu.CompilerParams(vmem_limit_bytes=20 * 1024 * 1024),
        cost_estimate=pl.CostEstimate(flops=4_000_000_000, bytes_accessed=8_000_000, transcendentals=0),
        name="early",
    )(*arrays)


def late_call(plane, *arrays):
    return pl.pallas_call(
        late_kernel,
        out_shape=(
            jax.ShapeDtypeStruct((8, C), F32),
            jax.ShapeDtypeStruct((plane, 1, C), F32),
        ) + results(1, 128),
        in_specs=[VMEM] * 6,
        out_specs=(VMEM,) * 5,
        scratch_shapes=[pltpu.VMEM((ROWS, C), F32)] + SCRATCH,
        compiler_params=pltpu.CompilerParams(vmem_limit_bytes=20 * 1024 * 1024),
        cost_estimate=pl.CostEstimate(flops=1_000_000_000, bytes_accessed=2_000_000, transcendentals=0),
        name="late",
    )(*arrays)


def relay_call(gathered, depth):
    return pl.pallas_call(
        relay_kernel,
        out_shape=jax.ShapeDtypeStruct((depth, 1, C), F32),
        in_specs=[VMEM],
        out_specs=VMEM,
        compiler_params=pltpu.CompilerParams(vmem_limit_bytes=4 * 1024 * 1024),
        name="relay",
    )(gathered)


def backward_call(*arrays):
    return pl.pallas_call(
        backward_kernel,
        out_shape=(jax.ShapeDtypeStruct((4, 8, C), F32), jax.ShapeDtypeStruct((8, C), F32)),
        in_specs=[VMEM] * 8,
        out_specs=(VMEM,) * 2,
        scratch_shapes=[pltpu.VMEM((3, C, C), F32), pltpu.VMEM((3, 8, C), F32)],
        compiler_params=pltpu.CompilerParams(vmem_limit_bytes=20 * 1024 * 1024),
        cost_estimate=pl.CostEstimate(flops=4_000_000_000, bytes_accessed=8_000_000, transcendentals=0),
        name="backward",
    )(*arrays)


def ring(size, step):
    return [(i, (i + step) % size) for i in range(size)]


def on_device(features, positions, occupied, neighbours, radial_weight, mix_weight, out_weight, *, outer, inner):
    gy = outer + inner
    size_x = lax.axis_size("gx")
    size_y = lax.axis_size(gy)
    own = pack_call(jnp.transpose(features, (0, 1, 3, 2, 4)), positions, occupied, neighbours)
    right = lax.ppermute(own, "gx", ring(size_x, -1))
    up = lax.ppermute(jnp.concatenate([own[:, :2], right[:, :2]], axis=0), gy, ring(size_y, -1))
    shared = (radial_weight, mix_weight, out_weight[None])
    early, *first = early_call(own, right, *shared)
    plane = size_x * lax.axis_size(outer)
    energy, spread, *last = late_call(plane, first[0], up, early, *shared)
    gathered = lax.all_to_all(spread, ("gx",) + outer, 0, 0)
    near, send_up = backward_call(*first, *last, radial_weight, energy)
    gathered, near = lax.optimization_barrier((gathered, near))
    gathered = lax.all_to_all(relay_call(gathered, lax.axis_size(inner)), inner, 0, 0)
    from_down = lax.ppermute(send_up, gy, ring(size_y, 1))
    near = near.at[:, 0].add(from_down[:4])[:, :4]
    from_left = lax.ppermute(near, "gx", ring(size_x, 1))
    total_energy = jnp.sum(gathered)

    def column(block, place):
        return block[:, :, :64].reshape(4, 8, 4, 8)[:, :, place]

    first = column(near, 2) + column(from_left, 1)
    second = column(near, 0) + column(from_left, 3)
    cells = jnp.stack([first, second], axis=1)
    return cells[:3], cells[3], total_energy


def solution(mesh):
    size_x, size_y = mesh.shape["gx"], mesh.shape["gy"]
    depth = 16 if size_y % 16 == 0 else size_y // 2
    split = Mesh(mesh.devices.reshape(size_x, size_y // depth, depth), ("gx", "gya", "gyb"))
    outer, inner = ("gya",), ("gyb",)
    gy = outer + inner
    in_specs = (
        P("gx", gy, None, None, None),
        P(None, "gx", gy, None),
        P("gx", gy, None),
        P("gx", gy, None, None),
        P(),
        P(),
        P(),
    )
    out_specs = (P(None, "gx", gy, None), P("gx", gy, None), P())

    def program(*arrays):
        return on_device(*arrays, outer=outer, inner=inner)

    return jax.shard_map(
        program, mesh=split, in_specs=in_specs, out_specs=out_specs, check_vma=False
    )
```

```python
import math

import jax
import jax.numpy as jnp
from jax import lax
from jax.experimental import pallas as pl
from jax.experimental.pallas import tpu as pltpu
from jax.sharding import Mesh, PartitionSpec as P

C = 128
NB = 8
GROUPS = 4
ROWS = 32
LEAD = (0, 3, 3, 3, 5, 5, 5, 5, 5)
PLAIN = (4, 4, 4, 6, 6, 6, 6, 6)
PAIRED = (1, 1, 1, 2, 2, 2, 2, 2)
R3 = math.sqrt(3.0)
R5 = math.sqrt(5.0)
R15 = math.sqrt(15.0)
F32 = jnp.float32
BF16 = jnp.bfloat16
NT = (((1,), (1,)), ((), ()))


def pack_kernel(features, places, present, lists, out, low_out, positions, occupied, neighbours, done):
    moves = [
        pltpu.make_async_copy(source, target, done.at[i])
        for i, (source, target) in enumerate(
            (
                (places, positions),
                (present, occupied),
                (lists, neighbours),
                (features, out.at[:, :, 0:9]),
            )
        )
    ]
    for move in moves:
        move.start()
    for move in moves[:3]:
        move.wait()
    flat = [positions[axis, x] for axis in range(3) for x in range(2)]
    flat = flat + [occupied[x].astype(F32) for x in range(2)]
    flat = jnp.concatenate(flat, axis=0)
    flat = jnp.concatenate([flat, jnp.zeros((64, C - 8), F32)], axis=1)
    flat = jnp.concatenate([flat, jnp.zeros((64, C), F32)], axis=0).T[0:8]
    high = flat.astype(BF16).astype(F32)
    rest = flat - high
    middle = rest.astype(BF16).astype(F32)
    low = pltpu.roll((rest - middle), 2, 1)
    middle = pltpu.roll(middle, 1, 1)
    lane = lax.broadcasted_iota(jnp.int32, (8, C), 1)
    kind = jnp.where(lane < 64, lane & 15, 3)
    for x in range(2):
        for y in range(8):
            back = (C - (8 * x + y)) % C
            codes = jnp.concatenate(
                [jnp.zeros((8, 64), F32), neighbours[x, y].astype(F32), jnp.zeros((8, 32), F32)], axis=1
            )
            tile = jnp.where(kind == 2, pltpu.roll(low, back, 1), codes)
            tile = jnp.where(kind == 1, pltpu.roll(middle, back, 1), tile)
            tile = jnp.where(kind == 0, pltpu.roll(high, back, 1), tile)
            out[x, y, 9] = tile.astype(BF16)
    moves[3].wait()
    low_out[...] = out[:, 0:2]


def count(codes):
    lanes = lax.broadcasted_iota(jnp.int32, (ROWS, C), 1).astype(F32)
    rows = lax.broadcasted_iota(jnp.int32, (ROWS, C), 0)
    code = codes.astype(jnp.int32)
    cell = code >> 3
    step_x = (cell * 11) >> 5
    x = ((rows >> 3) & 1) + step_x
    y = (rows >> 4) + cell - 3 * step_x
    column = jnp.where(x == 0, 2, jnp.where(x == 3, 3, x - 1))
    place = jnp.where(code < 72, (y * 4 + column) * 8 + (code & 7), -1).astype(F32)
    total = jnp.zeros((ROWS, C), F32)
    for k in range(32):
        total = total + jnp.where(lanes == place[:, 64 + k : 65 + k], 1.0, 0.0)
    return total


def block_of(q):
    return pl.ds(pl.multiple_of(q * 64, 64), C)


def weighted(products, weight, path):
    total = None
    for b in range(NB):
        term = weight[path, b : b + 1, :] * products[ROWS * b : ROWS * (b + 1)]
        total = term if total is None else total + term
    return total


def group_forward(table, weight, mix, out_weight, edge, back, energies, geometry, message):
    piece = lax.broadcasted_iota(jnp.int32, (16, C), 1)
    which = lax.broadcasted_iota(jnp.int32, (16, C), 0) * 16
    pick_rows = jnp.where((which < 64) & (piece >= which) & (piece < which + 3), 1.0, 0.0).astype(BF16)
    piece = lax.broadcasted_iota(jnp.int32, (C, 4 * C), 0)
    which = (lax.broadcasted_iota(jnp.int32, (C, 4 * C), 1) >> 7) * 16
    pick_columns = jnp.where((piece >= which) & (piece < which + 3), 1.0, 0.0).astype(BF16)
    lane = lax.broadcasted_iota(jnp.int32, (1, C), 1)
    column = (lane >> 3) & 3
    place_x = jnp.where(column == 2, 0, jnp.where(column == 3, 3, column + 1))
    shift_x = place_x.astype(F32) * 5.0
    shift_y = (lane >> 5).astype(F32) * 5.0
    row = lax.broadcasted_iota(jnp.int32, (ROWS, C), 0)
    own_shift_x = ((row >> 3) & 1).astype(F32) * 5.0 + 5.0
    own_shift_y = (row >> 4).astype(F32) * 5.0 + 5.0

    def group_values(q):
        base = pl.multiple_of(q * 64, 64)
        return jnp.concatenate(
            [
                table[pl.ds(base + 32, 16), 9 * C : 10 * C],
                table[pl.ds(base + 64, 16), 9 * C : 10 * C],
            ],
            axis=0,
        )

    def forward(q, carry):
        block = block_of(q)
        around = lax.dot_general(
            pick_rows, table[block, 9 * C : 10 * C], NT, preferred_element_type=F32
        )
        mine = group_values(q)
        own_at = jnp.dot(mine, pick_columns, preferred_element_type=F32)
        rx = (around[0:1] + shift_x) - (own_at[:, 0:C] + own_shift_x)
        ry = (around[1:2] + shift_y) - (own_at[:, C : 2 * C] + own_shift_y)
        rz = around[2:3] - own_at[:, 2 * C : 3 * C]
        times = count(mine.astype(F32))
        dist_sq = rx * rx + ry * ry + rz * rz
        inside = (times > 0.5) & (dist_sq < 25.0)
        dist_sq = jnp.where(inside, dist_sq, 25.0)
        fall = jnp.where(inside, 1.0 - dist_sq * 0.04, 0.0)
        inv = lax.rsqrt(dist_sq)
        inv = inv * (1.5 - 0.5 * dist_sq * inv * inv)
        turn = dist_sq * inv * (math.pi / 5.0) - math.pi / 2.0
        sq = turn * turn
        cosine = jnp.full_like(sq, 1.0 / math.factorial(12))
        for order in (10, 8, 6, 4, 2, 0):
            sign = 1.0 if order % 4 == 0 else -1.0
            cosine = cosine * sq + sign / math.factorial(order)
        sine = jnp.full_like(sq, 1.0 / math.factorial(13))
        for order in (11, 9, 7, 5, 3, 1):
            sign = 1.0 if order % 4 == 1 else -1.0
            sine = sine * sq + sign / math.factorial(order)
        s_now, c_now = cosine, -sine * turn
        twice = 2.0 * c_now
        s_last, c_last = jnp.zeros_like(sq), jnp.ones_like(sq)
        amount = times * around[3:4]
        base = amount * fall * fall * inv
        slope = -(amount * fall) * (fall * inv * inv + 0.16)
        ux, uy, uz = rx * inv, ry * inv, rz * inv
        harmonics = (
            None,
            R3 * ux,
            R3 * uy,
            R3 * uz,
            R15 * ux * uy,
            R15 * uy * uz,
            (0.5 * R5) * (3.0 * uz * uz - 1.0),
            R15 * ux * uz,
            (0.5 * R15) * (ux * ux - uy * uy),
        )
        edge[q, 0] = inv
        for g in range(1, 9):
            edge[q, g] = harmonics[g]
        for b in range(NB):
            radial = s_now * base
            edge[q, 9 + b] = radial
            edge[q, 17 + b] = c_now * base * ((b + 1) * math.pi / 5.0) + s_now * slope
            spot = slice(ROWS * b, ROWS * b + ROWS)
            geometry[0, spot] = radial.astype(BF16)
            for g in range(1, 9):
                geometry[g, spot] = (radial * harmonics[g]).astype(BF16)
            s_now, s_last = twice * s_now - s_last, s_now
            c_now, c_last = twice * c_now - c_last, c_now
        messages = [None] * 9
        for m in (0, 2, 4, 6, 8):
            width = 1 if m == 8 else 2
            products = jnp.dot(
                geometry[0], table[block, C * m : C * (m + width)], preferred_element_type=F32
            )
            for j in range(width):
                path = 0 if m + j == 0 else PLAIN[m + j - 1]
                messages[m + j] = weighted(products[:, C * j : C * j + C], weight, path)
        first = table[block, 0:C]
        for g in range(1, 9):
            both = jnp.concatenate([first, table[block, C * g : C * g + C]], axis=1)
            products = jnp.dot(geometry[g], both, preferred_element_type=F32)
            messages[g] = messages[g] + weighted(products[:, :C], weight, LEAD[g])
            messages[0] = messages[0] + weighted(products[:, C:], weight, PAIRED[g - 1])
        for g in range(9):
            message[g] = messages[g].astype(BF16)
        mixed = jnp.dot(message[...].reshape(9 * ROWS, C), mix[...], preferred_element_type=F32)
        mixed = mixed.reshape(9, ROWS, C)
        z = mixed[0]
        for g in range(1, 9):
            z = z + mixed[g] * mixed[g]
        gate = 1.0 / (1.0 + jnp.exp(-z))
        scale = own_at[:, 3 * C : 4 * C] * out_weight[0:1]
        spot = pl.ds(pl.multiple_of(q * ROWS, ROWS), ROWS)
        energies[spot] = scale * (z * gate)
        grad = scale * gate * (1.0 + z * (1.0 - gate))
        message[0] = grad.astype(BF16)
        grad = 2.0 * grad
        for g in range(1, 9):
            message[g] = (grad * mixed[g]).astype(BF16)
        returned = lax.dot_general(
            message[...].reshape(9 * ROWS, C), mix[...], NT, preferred_element_type=F32
        )
        back[q] = returned.reshape(9, ROWS, C)
        return carry

    return forward


def fill(table, row, m, tiles):
    rows = jnp.concatenate([tile.astype(F32) for tile in tiles], axis=0)
    table[32 * row : 32 * row + 32, C * m : C * m + C] = rows.astype(BF16)


def early_kernel(own, right, weight, mix, out_weight, energies, table, edge, back, geometry, message):
    for m in range(10):
        for y in range(8):
            fill(table, y, m, [own[1, y, m], right[0, y, m], own[0, y, m], right[1, y, m]])
    step = group_forward(table, weight, mix, out_weight, edge, back, energies, geometry, message)
    lax.fori_loop(0, GROUPS - 1, step, 0)


def late_kernel(
    known, up, across, early, weight, mix, out_weight,
    energy_out, spread_out, table, edge, back,
    energies, geometry, message,
):
    table[0:64] = known[192:256]
    for m in range(10):
        for y in range(2):
            fill(table, 2 + y, m, [up[1, y, m], across[0, y, m], up[0, y, m], across[1, y, m]])
    group_forward(table, weight, mix, out_weight, edge, back, energies, geometry, message)(0, 0)
    total = jnp.concatenate([early[...], energies[...]], axis=0)
    total = jnp.sum(total.T, axis=0, keepdims=True)
    energy_out[...] = jnp.broadcast_to(total, energy_out.shape)
    spread_out[...] = jnp.broadcast_to(total[None], spread_out.shape)


def stage_kernel(own, weight, mix, out_weight, own_copy, weight_copy, mix_copy, out_weight_copy):
    own_copy[...] = own[...]
    weight_copy[...] = weight[...]
    mix_copy[...] = mix[...]
    out_weight_copy[...] = out_weight[...]


def relay_kernel(gathered, out):
    total = jnp.sum(gathered[...], axis=0, keepdims=True)
    out[...] = jnp.broadcast_to(total, out.shape)


def group_backward(table, edge, back, weight, values, near, ahead):
    def backward(q, carry):
        block = block_of(q)
        first = table[block, 0:C]
        spot = pl.ds(pl.multiple_of((q + ahead) * ROWS, ROWS), ROWS)

        def spread(g, path):
            return jnp.concatenate(
                [(weight[path, b : b + 1, :] * back[q, g]).astype(BF16) for b in range(NB)], axis=0
            )

        wide = jnp.concatenate([spread(0, 0)] + [spread(g, PLAIN[g - 1]) for g in range(1, 9)], axis=1)
        grads = lax.dot_general(wide, table[block, 0 : 9 * C], NT, preferred_element_type=F32)
        along = [None] * NB
        sums = [None] * 9
        for b in range(NB):
            along[b] = grads[ROWS * b : ROWS * b + ROWS]
        paired = {1: spread(0, 1), 2: spread(0, 2)}
        for g in range(1, 9):
            both = jnp.concatenate([first, table[block, C * g : C * g + C]], axis=1)
            wide = jnp.concatenate([spread(g, LEAD[g]), paired[PAIRED[g - 1]]], axis=1)
            grads = lax.dot_general(wide, both, NT, preferred_element_type=F32)
            harmonic = edge[q, g]
            total = None
            for b in range(NB):
                part = grads[ROWS * b : ROWS * b + ROWS]
                along[b] = along[b] + part * harmonic
                term = part * edge[q, 9 + b]
                total = term if total is None else total + term
            sums[g] = total
        radial = None
        for b in range(NB):
            term = along[b] * edge[q, 17 + b]
            radial = term if radial is None else radial + term
        inv = edge[q, 0]
        ux, uy, uz = (edge[q, g] * (1.0 / R3) for g in (1, 2, 3))
        vx = R3 * sums[1] + R15 * (uy * sums[4] + uz * sums[7] + ux * sums[8])
        vy = R3 * sums[2] + R15 * (ux * sums[4] + uz * sums[5] - uy * sums[8])
        vz = R3 * sums[3] + R15 * (uy * sums[5] + ux * sums[7]) + (3.0 * R5) * uz * sums[6]
        inward = radial - inv * (ux * vx + uy * vy + uz * vz)
        for axis, (v, unit) in enumerate(((vx, ux), (vy, uy), (vz, uz))):
            gradient = inward * unit + inv * v
            values[axis, spot] = gradient
            near[axis, pl.ds(q + ahead, 1)] = jnp.sum(gradient, axis=0, keepdims=True)
        return carry

    return backward


def backward_kernel(
    table, edge, back, late_table, late_edge, late_back, weight, energy,
    near_out, send_up, values, near,
):
    near[...] = jnp.zeros_like(near)
    lax.fori_loop(0, GROUPS - 1, group_backward(table, edge, back, weight, values, near, 0), 0)
    group_backward(late_table, late_edge, late_back, weight, values, near, GROUPS - 1)(0, 0)
    send_up[...] = jnp.zeros_like(send_up)
    near_out[...] = jnp.zeros_like(near_out)
    lane = lax.broadcasted_iota(jnp.int32, (8, C), 1)
    for kind in range(4):
        if kind < 3:
            part = near[kind]
            later = pltpu.roll(pltpu.roll(part, 64, 1), 1, 0)
            pairs = -(part + later)
            own = jnp.sum(values[kind].T, axis=0, keepdims=True)
        else:
            pairs = jnp.zeros((8, C), F32)
            own = energy[0:1]
        own = jnp.concatenate(
            [own] + [pltpu.roll(own, C - 32 * q, 1) for q in range(1, 4)] + [jnp.zeros((4, C), F32)], axis=0
        )
        pairs = pairs + jnp.where((lane >= 32) & (lane < 48), pltpu.roll(own, 32, 1), 0.0)
        own = pltpu.roll(pltpu.roll(own, C - 16, 1), 1, 0)
        pairs = jnp.where(lane < 64, pairs + jnp.where(lane < 16, own, 0.0), 0.0)
        near_out[kind] = pairs
        send_up[kind : kind + 1] = pairs[4:5]


VMEM = pl.BlockSpec(memory_space=pltpu.VMEM)


def pack_call(features, positions, occupied, neighbours):
    return pl.pallas_call(
        pack_kernel,
        out_shape=(
            jax.ShapeDtypeStruct((2, 8, 10, 8, C), BF16),
            jax.ShapeDtypeStruct((2, 2, 10, 8, C), BF16),
        ),
        in_specs=[pl.BlockSpec(memory_space=pl.ANY)] * 4,
        out_specs=(VMEM, VMEM),
        scratch_shapes=[
            pltpu.VMEM(positions.shape, F32),
            pltpu.VMEM(occupied.shape, jnp.int32),
            pltpu.VMEM(neighbours.shape, jnp.int32),
            pltpu.SemaphoreType.DMA((4,)),
        ],
        name="pack",
    )(features, positions, occupied, neighbours)


def stage_call(*arrays):
    return pl.pallas_call(
        stage_kernel,
        out_shape=tuple(jax.ShapeDtypeStruct(a.shape, a.dtype) for a in arrays),
        in_specs=[VMEM] * 4,
        out_specs=(VMEM,) * 4,
        compiler_params=pltpu.CompilerParams(vmem_limit_bytes=8 * 1024 * 1024),
        cost_estimate=pl.CostEstimate(flops=2_000_000, bytes_accessed=2_000_000, transcendentals=0),
        name="stage",
    )(*arrays)


def results(groups, rows):
    return (
        jax.ShapeDtypeStruct((rows, 10 * C), BF16),
        jax.ShapeDtypeStruct((groups, 25, ROWS, C), F32),
        jax.ShapeDtypeStruct((groups, 9, ROWS, C), F32),
    )


SCRATCH = [pltpu.VMEM((9, NB * ROWS, C), BF16), pltpu.VMEM((9, ROWS, C), BF16)]


def early_call(*arrays):
    return pl.pallas_call(
        early_kernel,
        out_shape=(jax.ShapeDtypeStruct((3 * ROWS, C), F32),) + results(3, 256),
        in_specs=[VMEM] * 5,
        out_specs=(VMEM,) * 4,
        scratch_shapes=SCRATCH,
        compiler_params=pltpu.CompilerParams(vmem_limit_bytes=20 * 1024 * 1024),
        cost_estimate=pl.CostEstimate(flops=4_000_000_000, bytes_accessed=8_000_000, transcendentals=0),
        name="early",
    )(*arrays)


def late_call(plane, *arrays):
    return pl.pallas_call(
        late_kernel,
        out_shape=(
            jax.ShapeDtypeStruct((8, C), F32),
            jax.ShapeDtypeStruct((plane, 1, C), F32),
        ) + results(1, 128),
        in_specs=[VMEM] * 7,
        out_specs=(VMEM,) * 5,
        scratch_shapes=[pltpu.VMEM((ROWS, C), F32)] + SCRATCH,
        compiler_params=pltpu.CompilerParams(vmem_limit_bytes=20 * 1024 * 1024),
        cost_estimate=pl.CostEstimate(flops=1_000_000_000, bytes_accessed=2_000_000, transcendentals=0),
        name="late",
    )(*arrays)


def relay_call(gathered, depth):
    return pl.pallas_call(
        relay_kernel,
        out_shape=jax.ShapeDtypeStruct((depth, 1, C), F32),
        in_specs=[VMEM],
        out_specs=VMEM,
        compiler_params=pltpu.CompilerParams(vmem_limit_bytes=4 * 1024 * 1024),
        name="relay",
    )(gathered)


def backward_call(*arrays):
    return pl.pallas_call(
        backward_kernel,
        out_shape=(jax.ShapeDtypeStruct((4, 8, C), F32), jax.ShapeDtypeStruct((8, C), F32)),
        in_specs=[VMEM] * 8,
        out_specs=(VMEM,) * 2,
        scratch_shapes=[pltpu.VMEM((3, C, C), F32), pltpu.VMEM((3, 8, C), F32)],
        compiler_params=pltpu.CompilerParams(vmem_limit_bytes=20 * 1024 * 1024),
        cost_estimate=pl.CostEstimate(flops=4_000_000_000, bytes_accessed=8_000_000, transcendentals=0),
        name="backward",
    )(*arrays)


def ring(size, step):
    return [(i, (i + step) % size) for i in range(size)]


def on_device(features, positions, occupied, neighbours, radial_weight, mix_weight, out_weight, *, outer, inner):
    gy = outer + inner
    size_x = lax.axis_size("gx")
    size_y = lax.axis_size(gy)
    own, low = pack_call(jnp.transpose(features, (0, 1, 3, 2, 4)), positions, occupied, neighbours)
    right = lax.ppermute(own, "gx", ring(size_x, -1))
    up = lax.ppermute(low, gy, ring(size_y, -1))
    corner = [
        (x * size_y + y, (x - 1) % size_x * size_y + (y - 1) % size_y)
        for x in range(size_x)
        for y in range(size_y)
    ]
    across = lax.ppermute(low, ("gx",) + gy, corner)
    own, *shared = stage_call(own, radial_weight, mix_weight, out_weight[None])
    early, *first = early_call(own, right, *shared)
    plane = size_x * lax.axis_size(outer)
    energy, spread, *last = late_call(plane, first[0], up, across, early, *shared)
    gathered = lax.all_to_all(spread, ("gx",) + outer, 0, 0)
    near, send_up = backward_call(*first, *last, shared[0], energy)
    spread, send_up = lax.optimization_barrier((relay_call(gathered, lax.axis_size(inner)), send_up))
    gathered = lax.all_to_all(spread, inner, 0, 0)
    from_down = lax.ppermute(send_up, gy, ring(size_y, 1))
    near = near.at[:, 0].add(from_down[:4])[:, :4]
    from_left = lax.ppermute(near, "gx", ring(size_x, 1))
    total_energy = jnp.sum(gathered)

    def column(block, place):
        return block[:, :, :64].reshape(4, 8, 4, 8)[:, :, place]

    first = column(near, 2) + column(from_left, 1)
    second = column(near, 0) + column(from_left, 3)
    cells = jnp.stack([first, second], axis=1)
    return cells[:3], cells[3], total_energy


def solution(mesh):
    size_x, size_y = mesh.shape["gx"], mesh.shape["gy"]
    depth = 16 if size_y % 16 == 0 else size_y // 2
    split = Mesh(mesh.devices.reshape(size_x, size_y // depth, depth), ("gx", "gya", "gyb"))
    outer, inner = ("gya",), ("gyb",)
    gy = outer + inner
    in_specs = (
        P("gx", gy, None, None, None),
        P(None, "gx", gy, None),
        P("gx", gy, None),
        P("gx", gy, None, None),
        P(),
        P(),
        P(),
    )
    out_specs = (P(None, "gx", gy, None), P("gx", gy, None), P())

    def program(*arrays):
        return on_device(*arrays, outer=outer, inner=inner)

    return jax.shard_map(
        program, mesh=split, in_specs=in_specs, out_specs=out_specs, check_vma=False
    )
```

```python
import math

import jax
import jax.numpy as jnp
from jax import lax
from jax.experimental import pallas as pl
from jax.experimental.pallas import tpu as pltpu
from jax.sharding import Mesh, PartitionSpec as P

C = 128
NB = 8
GROUPS = 4
ROWS = 32
LEAD = (0, 3, 3, 3, 5, 5, 5, 5, 5)
PLAIN = (4, 4, 4, 6, 6, 6, 6, 6)
PAIRED = (1, 1, 1, 2, 2, 2, 2, 2)
R3 = math.sqrt(3.0)
R5 = math.sqrt(5.0)
R15 = math.sqrt(15.0)
F32 = jnp.float32
BF16 = jnp.bfloat16
NT = (((1,), (1,)), ((), ()))


def pack_kernel(
    features, places, present, lists, weight, out_weight, mix,
    out, low_out, shared, positions, occupied, neighbours, mix_copy, done,
):
    moves = [
        pltpu.make_async_copy(source, target, done.at[i])
        for i, (source, target) in enumerate(
            (
                (places, positions),
                (present, occupied),
                (lists, neighbours),
                (features, out.at[:, :, 0:9]),
                (weight, shared.at[0:7]),
                (out_weight, shared.at[7, 0:1]),
                (mix, mix_copy),
            )
        )
    ]
    for move in moves:
        move.start()
    for move in moves[:3]:
        move.wait()
    flat = [positions[axis, x] for axis in range(3) for x in range(2)]
    flat = flat + [occupied[x].astype(F32) for x in range(2)]
    flat = jnp.concatenate(flat, axis=0)
    flat = jnp.concatenate([flat, jnp.zeros((64, C - 8), F32)], axis=1)
    flat = jnp.concatenate([flat, jnp.zeros((64, C), F32)], axis=0).T[0:8]
    high = flat.astype(BF16).astype(F32)
    rest = flat - high
    middle = rest.astype(BF16).astype(F32)
    low = pltpu.roll((rest - middle), 2, 1)
    middle = pltpu.roll(middle, 1, 1)
    lane = lax.broadcasted_iota(jnp.int32, (8, C), 1)
    kind = jnp.where(lane < 64, lane & 15, 3)
    for x in range(2):
        for y in range(8):
            back = (C - (8 * x + y)) % C
            codes = jnp.concatenate(
                [jnp.zeros((8, 64), F32), neighbours[x, y].astype(F32), jnp.zeros((8, 32), F32)], axis=1
            )
            tile = jnp.where(kind == 2, pltpu.roll(low, back, 1), codes)
            tile = jnp.where(kind == 1, pltpu.roll(middle, back, 1), tile)
            tile = jnp.where(kind == 0, pltpu.roll(high, back, 1), tile)
            out[x, y, 9] = tile.astype(BF16)
    for move in moves[3:]:
        move.wait()
    shared[8:24] = mix_copy[...].astype(F32).reshape(16, 8, C)
    low_out[...] = out[:, 0:2]


def count(codes):
    lanes = lax.broadcasted_iota(jnp.int32, (ROWS, C), 1).astype(F32)
    rows = lax.broadcasted_iota(jnp.int32, (ROWS, C), 0)
    code = codes.astype(jnp.int32)
    cell = code >> 3
    step_x = (cell * 11) >> 5
    x = ((rows >> 3) & 1) + step_x
    y = (rows >> 4) + cell - 3 * step_x
    column = jnp.where(x == 0, 2, jnp.where(x == 3, 3, x - 1))
    place = jnp.where(code < 72, (y * 4 + column) * 8 + (code & 7), -1).astype(F32)
    total = jnp.zeros((ROWS, C), F32)
    for k in range(32):
        total = total + jnp.where(lanes == place[:, 64 + k : 65 + k], 1.0, 0.0)
    return total


def block_of(q):
    return pl.ds(pl.multiple_of(q * 64, 64), C)


def weighted(products, weight, path):
    total = None
    for b in range(NB):
        term = weight[path, b : b + 1, :] * products[ROWS * b : ROWS * (b + 1)]
        total = term if total is None else total + term
    return total


def group_forward(table, weight, mix, out_weight, edge, back, energies, geometry, message):
    piece = lax.broadcasted_iota(jnp.int32, (16, C), 1)
    which = lax.broadcasted_iota(jnp.int32, (16, C), 0) * 16
    pick_rows = jnp.where((which < 64) & (piece >= which) & (piece < which + 3), 1.0, 0.0).astype(BF16)
    piece = lax.broadcasted_iota(jnp.int32, (C, 4 * C), 0)
    which = (lax.broadcasted_iota(jnp.int32, (C, 4 * C), 1) >> 7) * 16
    pick_columns = jnp.where((piece >= which) & (piece < which + 3), 1.0, 0.0).astype(BF16)
    lane = lax.broadcasted_iota(jnp.int32, (1, C), 1)
    column = (lane >> 3) & 3
    place_x = jnp.where(column == 2, 0, jnp.where(column == 3, 3, column + 1))
    shift_x = place_x.astype(F32) * 5.0
    shift_y = (lane >> 5).astype(F32) * 5.0
    row = lax.broadcasted_iota(jnp.int32, (ROWS, C), 0)
    own_shift_x = ((row >> 3) & 1).astype(F32) * 5.0 + 5.0
    own_shift_y = (row >> 4).astype(F32) * 5.0 + 5.0

    def group_values(q):
        base = pl.multiple_of(q * 64, 64)
        return jnp.concatenate(
            [
                table[pl.ds(base + 32, 16), 9 * C : 10 * C],
                table[pl.ds(base + 64, 16), 9 * C : 10 * C],
            ],
            axis=0,
        )

    def forward(q, carry):
        block = block_of(q)
        around = lax.dot_general(
            pick_rows, table[block, 9 * C : 10 * C], NT, preferred_element_type=F32
        )
        mine = group_values(q)
        own_at = jnp.dot(mine, pick_columns, preferred_element_type=F32)
        rx = (around[0:1] + shift_x) - (own_at[:, 0:C] + own_shift_x)
        ry = (around[1:2] + shift_y) - (own_at[:, C : 2 * C] + own_shift_y)
        rz = around[2:3] - own_at[:, 2 * C : 3 * C]
        times = count(mine.astype(F32))
        dist_sq = rx * rx + ry * ry + rz * rz
        inside = (times > 0.5) & (dist_sq < 25.0)
        dist_sq = jnp.where(inside, dist_sq, 25.0)
        fall = jnp.where(inside, 1.0 - dist_sq * 0.04, 0.0)
        inv = lax.rsqrt(dist_sq)
        inv = inv * (1.5 - 0.5 * dist_sq * inv * inv)
        turn = dist_sq * inv * (math.pi / 5.0) - math.pi / 2.0
        sq = turn * turn
        cosine = jnp.full_like(sq, 1.0 / math.factorial(12))
        for order in (10, 8, 6, 4, 2, 0):
            sign = 1.0 if order % 4 == 0 else -1.0
            cosine = cosine * sq + sign / math.factorial(order)
        sine = jnp.full_like(sq, 1.0 / math.factorial(13))
        for order in (11, 9, 7, 5, 3, 1):
            sign = 1.0 if order % 4 == 1 else -1.0
            sine = sine * sq + sign / math.factorial(order)
        s_now, c_now = cosine, -sine * turn
        twice = 2.0 * c_now
        s_last, c_last = jnp.zeros_like(sq), jnp.ones_like(sq)
        amount = times * around[3:4]
        base = amount * fall * fall * inv
        slope = -(amount * fall) * (fall * inv * inv + 0.16)
        ux, uy, uz = rx * inv, ry * inv, rz * inv
        harmonics = (
            None,
            R3 * ux,
            R3 * uy,
            R3 * uz,
            R15 * ux * uy,
            R15 * uy * uz,
            (0.5 * R5) * (3.0 * uz * uz - 1.0),
            R15 * ux * uz,
            (0.5 * R15) * (ux * ux - uy * uy),
        )
        edge[q, 0] = inv
        for g in range(1, 9):
            edge[q, g] = harmonics[g]
        for b in range(NB):
            radial = s_now * base
            edge[q, 9 + b] = radial
            edge[q, 17 + b] = c_now * base * ((b + 1) * math.pi / 5.0) + s_now * slope
            spot = slice(ROWS * b, ROWS * b + ROWS)
            geometry[0, spot] = radial.astype(BF16)
            for g in range(1, 9):
                geometry[g, spot] = (radial * harmonics[g]).astype(BF16)
            s_now, s_last = twice * s_now - s_last, s_now
            c_now, c_last = twice * c_now - c_last, c_now
        messages = [None] * 9
        for m in (0, 2, 4, 6, 8):
            width = 1 if m == 8 else 2
            products = jnp.dot(
                geometry[0], table[block, C * m : C * (m + width)], preferred_element_type=F32
            )
            for j in range(width):
                path = 0 if m + j == 0 else PLAIN[m + j - 1]
                messages[m + j] = weighted(products[:, C * j : C * j + C], weight, path)
        first = table[block, 0:C]
        for g in range(1, 9):
            both = jnp.concatenate([first, table[block, C * g : C * g + C]], axis=1)
            products = jnp.dot(geometry[g], both, preferred_element_type=F32)
            messages[g] = messages[g] + weighted(products[:, :C], weight, LEAD[g])
            messages[0] = messages[0] + weighted(products[:, C:], weight, PAIRED[g - 1])
        for g in range(9):
            message[g] = messages[g].astype(BF16)
        mixed = jnp.dot(message[...].reshape(9 * ROWS, C), mix[...], preferred_element_type=F32)
        mixed = mixed.reshape(9, ROWS, C)
        z = mixed[0]
        for g in range(1, 9):
            z = z + mixed[g] * mixed[g]
        gate = 1.0 / (1.0 + jnp.exp(-z))
        scale = own_at[:, 3 * C : 4 * C] * out_weight[0:1]
        spot = pl.ds(pl.multiple_of(q * ROWS, ROWS), ROWS)
        energies[spot] = scale * (z * gate)
        grad = scale * gate * (1.0 + z * (1.0 - gate))
        message[0] = grad.astype(BF16)
        grad = 2.0 * grad
        for g in range(1, 9):
            message[g] = (grad * mixed[g]).astype(BF16)
        returned = lax.dot_general(
            message[...].reshape(9 * ROWS, C), mix[...], NT, preferred_element_type=F32
        )
        back[q] = returned.reshape(9, ROWS, C)
        return carry

    return forward


def fill(table, row, m, tiles):
    rows = jnp.concatenate([tile.astype(F32) for tile in tiles], axis=0)
    table[32 * row : 32 * row + 32, C * m : C * m + C] = rows.astype(BF16)


def early_kernel(own, right, weight, mix, out_weight, energies, table, edge, back, geometry, message):
    for m in range(10):
        for y in range(8):
            fill(table, y, m, [own[1, y, m], right[0, y, m], own[0, y, m], right[1, y, m]])
    step = group_forward(table, weight, mix, out_weight, edge, back, energies, geometry, message)
    lax.fori_loop(0, GROUPS - 1, step, 0)


def late_kernel(
    known, up, across, early, weight, mix, out_weight,
    energy_out, spread_out, table, edge, back,
    energies, geometry, message,
):
    table[0:64] = known[192:256]
    for m in range(10):
        for y in range(2):
            fill(table, 2 + y, m, [up[1, y, m], across[0, y, m], up[0, y, m], across[1, y, m]])
    group_forward(table, weight, mix, out_weight, edge, back, energies, geometry, message)(0, 0)
    total = jnp.concatenate([early[...], energies[...]], axis=0)
    total = jnp.sum(total.T, axis=0, keepdims=True)
    energy_out[...] = jnp.broadcast_to(total, energy_out.shape)
    spread_out[...] = jnp.broadcast_to(total[None], spread_out.shape)


def stage_kernel(own, shared, own_copy, weight, mix, out_weight):
    own_copy[...] = own[...]
    weight[...] = shared[0:7]
    out_weight[...] = shared[7, 0:1]
    mix[...] = shared[8:24].reshape(C, C).astype(BF16)


def relay_kernel(gathered, out):
    total = jnp.sum(gathered[...], axis=0, keepdims=True)
    out[...] = jnp.broadcast_to(total, out.shape)


def group_backward(table, edge, back, weight, values, near, ahead):
    def backward(q, carry):
        block = block_of(q)
        first = table[block, 0:C]
        spot = pl.ds(pl.multiple_of((q + ahead) * ROWS, ROWS), ROWS)

        def spread(g, path):
            return jnp.concatenate(
                [(weight[path, b : b + 1, :] * back[q, g]).astype(BF16) for b in range(NB)], axis=0
            )

        wide = jnp.concatenate([spread(0, 0)] + [spread(g, PLAIN[g - 1]) for g in range(1, 9)], axis=1)
        grads = lax.dot_general(wide, table[block, 0 : 9 * C], NT, preferred_element_type=F32)
        along = [None] * NB
        sums = [None] * 9
        for b in range(NB):
            along[b] = grads[ROWS * b : ROWS * b + ROWS]
        paired = {1: spread(0, 1), 2: spread(0, 2)}
        for g in range(1, 9):
            both = jnp.concatenate([first, table[block, C * g : C * g + C]], axis=1)
            wide = jnp.concatenate([spread(g, LEAD[g]), paired[PAIRED[g - 1]]], axis=1)
            grads = lax.dot_general(wide, both, NT, preferred_element_type=F32)
            harmonic = edge[q, g]
            total = None
            for b in range(NB):
                part = grads[ROWS * b : ROWS * b + ROWS]
                along[b] = along[b] + part * harmonic
                term = part * edge[q, 9 + b]
                total = term if total is None else total + term
            sums[g] = total
        radial = None
        for b in range(NB):
            term = along[b] * edge[q, 17 + b]
            radial = term if radial is None else radial + term
        inv = edge[q, 0]
        ux, uy, uz = (edge[q, g] * (1.0 / R3) for g in (1, 2, 3))
        vx = R3 * sums[1] + R15 * (uy * sums[4] + uz * sums[7] + ux * sums[8])
        vy = R3 * sums[2] + R15 * (ux * sums[4] + uz * sums[5] - uy * sums[8])
        vz = R3 * sums[3] + R15 * (uy * sums[5] + ux * sums[7]) + (3.0 * R5) * uz * sums[6]
        inward = radial - inv * (ux * vx + uy * vy + uz * vz)
        for axis, (v, unit) in enumerate(((vx, ux), (vy, uy), (vz, uz))):
            gradient = inward * unit + inv * v
            values[axis, spot] = gradient
            near[axis, pl.ds(q + ahead, 1)] = jnp.sum(gradient, axis=0, keepdims=True)
        return carry

    return backward


def backward_kernel(
    table, edge, back, late_table, late_edge, late_back, weight, energy,
    near_out, send_up, values, near,
):
    near[...] = jnp.zeros_like(near)
    lax.fori_loop(0, GROUPS - 1, group_backward(table, edge, back, weight, values, near, 0), 0)
    group_backward(late_table, late_edge, late_back, weight, values, near, GROUPS - 1)(0, 0)
    send_up[...] = jnp.zeros_like(send_up)
    near_out[...] = jnp.zeros_like(near_out)
    lane = lax.broadcasted_iota(jnp.int32, (8, C), 1)
    for kind in range(4):
        if kind < 3:
            part = near[kind]
            later = pltpu.roll(pltpu.roll(part, 64, 1), 1, 0)
            pairs = -(part + later)
            own = jnp.sum(values[kind].T, axis=0, keepdims=True)
        else:
            pairs = jnp.zeros((8, C), F32)
            own = energy[0:1]
        own = jnp.concatenate(
            [own] + [pltpu.roll(own, C - 32 * q, 1) for q in range(1, 4)] + [jnp.zeros((4, C), F32)], axis=0
        )
        pairs = pairs + jnp.where((lane >= 32) & (lane < 48), pltpu.roll(own, 32, 1), 0.0)
        own = pltpu.roll(pltpu.roll(own, C - 16, 1), 1, 0)
        pairs = jnp.where(lane < 64, pairs + jnp.where(lane < 16, own, 0.0), 0.0)
        near_out[kind] = pairs
        send_up[kind : kind + 1] = pairs[4:5]


def finish_kernel(near, from_left, from_down, from_across, forces, energies):
    row = lax.broadcasted_iota(jnp.int32, (8, C), 0)
    for kind in range(4):
        mine = near[kind] + jnp.where(row == 0, from_down[kind : kind + 1], 0.0)
        theirs = from_left[kind] + jnp.where(row == 0, from_across[kind : kind + 1], 0.0)
        columns = (
            pltpu.roll(mine, C - 16, 1) + pltpu.roll(theirs, C - 8, 1),
            mine + pltpu.roll(theirs, C - 24, 1),
        )
        for x in range(2):
            for odd in range(2):
                cells = columns[x] if odd == 0 else pltpu.roll(columns[x], C - 32, 1)
                for p in range(4):
                    y = 2 * p + odd
                    if kind < 3:
                        forces[kind, x, y : y + 1] = cells[p : p + 1, 0:8]
                    else:
                        energies[x, y : y + 1] = cells[p : p + 1, 0:8]


VMEM = pl.BlockSpec(memory_space=pltpu.VMEM)


def pack_call(features, positions, occupied, neighbours, *weights):
    return pl.pallas_call(
        pack_kernel,
        out_shape=(
            jax.ShapeDtypeStruct((2, 8, 10, 8, C), BF16),
            jax.ShapeDtypeStruct((2, 2, 10, 8, C), BF16),
            jax.ShapeDtypeStruct((24, 8, C), F32),
        ),
        in_specs=[pl.BlockSpec(memory_space=pl.ANY)] * 7,
        out_specs=(VMEM,) * 3,
        scratch_shapes=[
            pltpu.VMEM(positions.shape, F32),
            pltpu.VMEM(occupied.shape, jnp.int32),
            pltpu.VMEM(neighbours.shape, jnp.int32),
            pltpu.VMEM((C, C), BF16),
            pltpu.SemaphoreType.DMA((7,)),
        ],
        name="pack",
    )(features, positions, occupied, neighbours, *weights)


def stage_call(own, shared):
    return pl.pallas_call(
        stage_kernel,
        out_shape=(
            jax.ShapeDtypeStruct(own.shape, BF16),
            jax.ShapeDtypeStruct((7, NB, C), F32),
            jax.ShapeDtypeStruct((C, C), BF16),
            jax.ShapeDtypeStruct((1, C), F32),
        ),
        in_specs=[VMEM] * 2,
        out_specs=(VMEM,) * 4,
        compiler_params=pltpu.CompilerParams(vmem_limit_bytes=8 * 1024 * 1024),
        cost_estimate=pl.CostEstimate(flops=2_000_000, bytes_accessed=2_000_000, transcendentals=0),
        name="stage",
    )(own, shared)


def results(groups, rows):
    return (
        jax.ShapeDtypeStruct((rows, 10 * C), BF16),
        jax.ShapeDtypeStruct((groups, 25, ROWS, C), F32),
        jax.ShapeDtypeStruct((groups, 9, ROWS, C), F32),
    )


SCRATCH = [pltpu.VMEM((9, NB * ROWS, C), BF16), pltpu.VMEM((9, ROWS, C), BF16)]


def early_call(*arrays):
    return pl.pallas_call(
        early_kernel,
        out_shape=(jax.ShapeDtypeStruct((3 * ROWS, C), F32),) + results(3, 256),
        in_specs=[VMEM] * 5,
        out_specs=(VMEM,) * 4,
        scratch_shapes=SCRATCH,
        compiler_params=pltpu.CompilerParams(vmem_limit_bytes=20 * 1024 * 1024),
        cost_estimate=pl.CostEstimate(flops=4_000_000_000, bytes_accessed=8_000_000, transcendentals=0),
        name="early",
    )(*arrays)


def late_call(plane, *arrays):
    return pl.pallas_call(
        late_kernel,
        out_shape=(
            jax.ShapeDtypeStruct((8, C), F32),
            jax.ShapeDtypeStruct((plane, 1, C), F32),
        ) + results(1, 128),
        in_specs=[VMEM] * 7,
        out_specs=(VMEM,) * 5,
        scratch_shapes=[pltpu.VMEM((ROWS, C), F32)] + SCRATCH,
        compiler_params=pltpu.CompilerParams(vmem_limit_bytes=20 * 1024 * 1024),
        cost_estimate=pl.CostEstimate(flops=1_000_000_000, bytes_accessed=2_000_000, transcendentals=0),
        name="late",
    )(*arrays)


def relay_call(gathered, depth):
    return pl.pallas_call(
        relay_kernel,
        out_shape=jax.ShapeDtypeStruct((depth, 1, C), F32),
        in_specs=[VMEM],
        out_specs=VMEM,
        compiler_params=pltpu.CompilerParams(vmem_limit_bytes=4 * 1024 * 1024),
        name="relay",
    )(gathered)


def backward_call(*arrays):
    return pl.pallas_call(
        backward_kernel,
        out_shape=(jax.ShapeDtypeStruct((4, 8, C), F32), jax.ShapeDtypeStruct((8, C), F32)),
        in_specs=[VMEM] * 8,
        out_specs=(VMEM,) * 2,
        scratch_shapes=[pltpu.VMEM((3, C, C), F32), pltpu.VMEM((3, 8, C), F32)],
        compiler_params=pltpu.CompilerParams(vmem_limit_bytes=20 * 1024 * 1024),
        cost_estimate=pl.CostEstimate(flops=4_000_000_000, bytes_accessed=8_000_000, transcendentals=0),
        name="backward",
    )(*arrays)


def finish_call(*arrays):
    return pl.pallas_call(
        finish_kernel,
        out_shape=(
            jax.ShapeDtypeStruct((3, 2, 8, 8), F32),
            jax.ShapeDtypeStruct((2, 8, 8), F32),
        ),
        in_specs=[VMEM] * 4,
        out_specs=(VMEM,) * 2,
        compiler_params=pltpu.CompilerParams(vmem_limit_bytes=4 * 1024 * 1024),
        cost_estimate=pl.CostEstimate(flops=1000, bytes_accessed=1000, transcendentals=0),
        name="finish",
    )(*arrays)


def ring(size, step):
    return [(i, (i + step) % size) for i in range(size)]


def on_device(features, positions, occupied, neighbours, radial_weight, mix_weight, out_weight, *, outer, inner):
    gy = outer + inner
    size_x = lax.axis_size("gx")
    size_y = lax.axis_size(gy)
    own, low, shared = pack_call(
        jnp.transpose(features, (0, 1, 3, 2, 4)), positions, occupied, neighbours,
        radial_weight, out_weight[None], mix_weight,
    )
    right = lax.ppermute(own, "gx", ring(size_x, -1))
    up = lax.ppermute(low, gy, ring(size_y, -1))
    corner = [
        (x * size_y + y, (x - 1) % size_x * size_y + (y - 1) % size_y)
        for x in range(size_x)
        for y in range(size_y)
    ]
    across = lax.ppermute(low, ("gx",) + gy, corner)
    own, *shared = stage_call(own, shared)
    early, *first = early_call(own, right, *shared)
    plane = size_x * lax.axis_size(outer)
    energy, spread, *last = late_call(plane, first[0], up, across, early, *shared)
    gathered = lax.all_to_all(spread, ("gx",) + outer, 0, 0)
    near, send_up = backward_call(*first, *last, shared[0], energy)
    spread = relay_call(gathered, lax.axis_size(inner))
    spread, near, send_up = lax.optimization_barrier((spread, near, send_up))
    gathered = lax.all_to_all(spread, inner, 0, 0)
    from_left = lax.ppermute(near, "gx", ring(size_x, 1))
    from_down = lax.ppermute(send_up, gy, ring(size_y, 1))
    from_across = lax.ppermute(send_up, ("gx",) + gy, [(j, i) for i, j in corner])
    forces, slot_energy_values = finish_call(near, from_left, from_down, from_across)
    return forces, slot_energy_values, jnp.sum(gathered)


def solution(mesh):
    size_x, size_y = mesh.shape["gx"], mesh.shape["gy"]
    depth = 16 if size_y % 16 == 0 else size_y // 2
    split = Mesh(mesh.devices.reshape(size_x, size_y // depth, depth), ("gx", "gya", "gyb"))
    outer, inner = ("gya",), ("gyb",)
    gy = outer + inner
    in_specs = (
        P("gx", gy, None, None, None),
        P(None, "gx", gy, None),
        P("gx", gy, None),
        P("gx", gy, None, None),
        P(),
        P(),
        P(),
    )
    out_specs = (P(None, "gx", gy, None), P("gx", gy, None), P())

    def program(*arrays):
        return on_device(*arrays, outer=outer, inner=inner)

    return jax.shard_map(
        program, mesh=split, in_specs=in_specs, out_specs=out_specs, check_vma=False
    )
```

```python
import math

import jax
import jax.numpy as jnp
from jax import lax
from jax.experimental import pallas as pl
from jax.experimental.pallas import tpu as pltpu
from jax.sharding import Mesh, PartitionSpec as P

C = 128
NB = 8
GROUPS = 4
ROWS = 32
LEAD = (0, 3, 3, 3, 5, 5, 5, 5, 5)
PLAIN = (4, 4, 4, 6, 6, 6, 6, 6)
PAIRED = (1, 1, 1, 2, 2, 2, 2, 2)
R3 = math.sqrt(3.0)
R5 = math.sqrt(5.0)
R15 = math.sqrt(15.0)
F32 = jnp.float32
BF16 = jnp.bfloat16
NT = (((1,), (1,)), ((), ()))


def pack_kernel(
    features, places, present, lists, weight, out_weight, mix,
    out, low_out, shared, positions, occupied, neighbours, mix_copy, done,
):
    moves = [
        pltpu.make_async_copy(source, target, done.at[i])
        for i, (source, target) in enumerate(
            (
                (places, positions),
                (present, occupied),
                (lists, neighbours),
                (features, out.at[:, :, 0:9]),
                (weight, shared.at[0:7]),
                (out_weight, shared.at[7, 0:1]),
                (mix, mix_copy),
            )
        )
    ]
    for move in moves:
        move.start()
    for move in moves[:3]:
        move.wait()
    flat = [positions[axis, x] for axis in range(3) for x in range(2)]
    flat = flat + [occupied[x].astype(F32) for x in range(2)]
    flat = jnp.concatenate(flat, axis=0)
    flat = jnp.concatenate([flat, jnp.zeros((64, C - 8), F32)], axis=1)
    flat = jnp.concatenate([flat, jnp.zeros((64, C), F32)], axis=0).T[0:8]
    high = flat.astype(BF16).astype(F32)
    rest = flat - high
    middle = rest.astype(BF16).astype(F32)
    low = pltpu.roll((rest - middle), 2, 1)
    middle = pltpu.roll(middle, 1, 1)
    lane = lax.broadcasted_iota(jnp.int32, (8, C), 1)
    kind = jnp.where(lane < 64, lane & 15, 3)
    for x in range(2):
        for y in range(8):
            back = (C - (8 * x + y)) % C
            codes = jnp.concatenate(
                [jnp.zeros((8, 64), F32), neighbours[x, y].astype(F32), jnp.zeros((8, 32), F32)], axis=1
            )
            tile = jnp.where(kind == 2, pltpu.roll(low, back, 1), codes)
            tile = jnp.where(kind == 1, pltpu.roll(middle, back, 1), tile)
            tile = jnp.where(kind == 0, pltpu.roll(high, back, 1), tile)
            out[x, y, 9] = tile.astype(BF16)
    for move in moves[3:]:
        move.wait()
    shared[8:24] = mix_copy[...].astype(F32).reshape(16, 8, C)
    low_out[...] = out[:, 0:2]


def count(codes):
    lanes = lax.broadcasted_iota(jnp.int32, (ROWS, C), 1).astype(F32)
    rows = lax.broadcasted_iota(jnp.int32, (ROWS, C), 0)
    code = codes.astype(jnp.int32)
    cell = code >> 3
    step_x = (cell * 11) >> 5
    x = ((rows >> 3) & 1) + step_x
    y = (rows >> 4) + cell - 3 * step_x
    column = jnp.where(x == 0, 2, jnp.where(x == 3, 3, x - 1))
    place = jnp.where(code < 72, (y * 4 + column) * 8 + (code & 7), -1).astype(F32)
    total = jnp.zeros((ROWS, C), F32)
    for k in range(32):
        total = total + jnp.where(lanes == place[:, 64 + k : 65 + k], 1.0, 0.0)
    return total


def block_of(q):
    return pl.ds(pl.multiple_of(q * 64, 64), C)


def weighted(products, weight, path):
    total = None
    for b in range(NB):
        term = weight[path, b : b + 1, :] * products[ROWS * b : ROWS * (b + 1)]
        total = term if total is None else total + term
    return total


def group_forward(table, weight, mix, out_weight, edge, back, energies, geometry, message):
    piece = lax.broadcasted_iota(jnp.int32, (16, C), 1)
    which = lax.broadcasted_iota(jnp.int32, (16, C), 0) * 16
    pick_rows = jnp.where((which < 64) & (piece >= which) & (piece < which + 3), 1.0, 0.0).astype(BF16)
    piece = lax.broadcasted_iota(jnp.int32, (C, 4 * C), 0)
    which = (lax.broadcasted_iota(jnp.int32, (C, 4 * C), 1) >> 7) * 16
    pick_columns = jnp.where((piece >= which) & (piece < which + 3), 1.0, 0.0).astype(BF16)
    lane = lax.broadcasted_iota(jnp.int32, (1, C), 1)
    column = (lane >> 3) & 3
    place_x = jnp.where(column == 2, 0, jnp.where(column == 3, 3, column + 1))
    shift_x = place_x.astype(F32) * 5.0
    shift_y = (lane >> 5).astype(F32) * 5.0
    row = lax.broadcasted_iota(jnp.int32, (ROWS, C), 0)
    own_shift_x = ((row >> 3) & 1).astype(F32) * 5.0 + 5.0
    own_shift_y = (row >> 4).astype(F32) * 5.0 + 5.0

    def group_values(q):
        base = pl.multiple_of(q * 64, 64)
        return jnp.concatenate(
            [
                table[pl.ds(base + 32, 16), 9 * C : 10 * C],
                table[pl.ds(base + 64, 16), 9 * C : 10 * C],
            ],
            axis=0,
        )

    def forward(q, carry):
        block = block_of(q)
        around = lax.dot_general(
            pick_rows, table[block, 9 * C : 10 * C], NT, preferred_element_type=F32
        )
        mine = group_values(q)
        own_at = jnp.dot(mine, pick_columns, preferred_element_type=F32)
        rx = (around[0:1] + shift_x) - (own_at[:, 0:C] + own_shift_x)
        ry = (around[1:2] + shift_y) - (own_at[:, C : 2 * C] + own_shift_y)
        rz = around[2:3] - own_at[:, 2 * C : 3 * C]
        times = count(mine.astype(F32))
        dist_sq = rx * rx + ry * ry + rz * rz
        inside = (times > 0.5) & (dist_sq < 25.0)
        dist_sq = jnp.where(inside, dist_sq, 25.0)
        fall = jnp.where(inside, 1.0 - dist_sq * 0.04, 0.0)
        inv = lax.rsqrt(dist_sq)
        inv = inv * (1.5 - 0.5 * dist_sq * inv * inv)
        turn = dist_sq * inv * (math.pi / 5.0) - math.pi / 2.0
        sq = turn * turn
        cosine = jnp.full_like(sq, 1.0 / math.factorial(12))
        for order in (10, 8, 6, 4, 2, 0):
            sign = 1.0 if order % 4 == 0 else -1.0
            cosine = cosine * sq + sign / math.factorial(order)
        sine = jnp.full_like(sq, 1.0 / math.factorial(13))
        for order in (11, 9, 7, 5, 3, 1):
            sign = 1.0 if order % 4 == 1 else -1.0
            sine = sine * sq + sign / math.factorial(order)
        s_now, c_now = cosine, -sine * turn
        twice = 2.0 * c_now
        s_last, c_last = jnp.zeros_like(sq), jnp.ones_like(sq)
        amount = times * around[3:4]
        base = amount * fall * fall * inv
        slope = -(amount * fall) * (fall * inv * inv + 0.16)
        ux, uy, uz = rx * inv, ry * inv, rz * inv
        harmonics = (
            None,
            R3 * ux,
            R3 * uy,
            R3 * uz,
            R15 * ux * uy,
            R15 * uy * uz,
            (0.5 * R5) * (3.0 * uz * uz - 1.0),
            R15 * ux * uz,
            (0.5 * R15) * (ux * ux - uy * uy),
        )
        edge[q, 0] = inv
        for g in range(1, 9):
            edge[q, g] = harmonics[g]
        for b in range(NB):
            radial = s_now * base
            edge[q, 9 + b] = radial
            edge[q, 17 + b] = c_now * base * ((b + 1) * math.pi / 5.0) + s_now * slope
            spot = slice(ROWS * b, ROWS * b + ROWS)
            geometry[0, spot] = radial.astype(BF16)
            for g in range(1, 9):
                geometry[g, spot] = (radial * harmonics[g]).astype(BF16)
            s_now, s_last = twice * s_now - s_last, s_now
            c_now, c_last = twice * c_now - c_last, c_now
        messages = [None] * 9
        for m in (0, 2, 4, 6, 8):
            width = 1 if m == 8 else 2
            products = jnp.dot(
                geometry[0], table[block, C * m : C * (m + width)], preferred_element_type=F32
            )
            for j in range(width):
                path = 0 if m + j == 0 else PLAIN[m + j - 1]
                messages[m + j] = weighted(products[:, C * j : C * j + C], weight, path)
        first = table[block, 0:C]
        for g in range(1, 9):
            both = jnp.concatenate([first, table[block, C * g : C * g + C]], axis=1)
            products = jnp.dot(geometry[g], both, preferred_element_type=F32)
            messages[g] = messages[g] + weighted(products[:, :C], weight, LEAD[g])
            messages[0] = messages[0] + weighted(products[:, C:], weight, PAIRED[g - 1])
        for g in range(9):
            message[g] = messages[g].astype(BF16)
        mixed = jnp.dot(message[...].reshape(9 * ROWS, C), mix[...], preferred_element_type=F32)
        mixed = mixed.reshape(9, ROWS, C)
        z = mixed[0]
        for g in range(1, 9):
            z = z + mixed[g] * mixed[g]
        gate = 1.0 / (1.0 + jnp.exp(-z))
        scale = own_at[:, 3 * C : 4 * C] * out_weight[0:1]
        spot = pl.ds(pl.multiple_of(q * ROWS, ROWS), ROWS)
        energies[spot] = scale * (z * gate)
        grad = scale * gate * (1.0 + z * (1.0 - gate))
        message[0] = grad.astype(BF16)
        grad = 2.0 * grad
        for g in range(1, 9):
            message[g] = (grad * mixed[g]).astype(BF16)
        returned = lax.dot_general(
            message[...].reshape(9 * ROWS, C), mix[...], NT, preferred_element_type=F32
        )
        back[q] = returned.reshape(9, ROWS, C)
        return carry

    return forward


def fill(table, row, m, tiles):
    rows = jnp.concatenate([tile.astype(F32) for tile in tiles], axis=0)
    table[32 * row : 32 * row + 32, C * m : C * m + C] = rows.astype(BF16)


def early_kernel(own, right, weight, mix, out_weight, energies, table, edge, back, geometry, message):
    for m in range(10):
        for y in range(8):
            fill(table, y, m, [own[1, y, m], right[0, y, m], own[0, y, m], right[1, y, m]])
    step = group_forward(table, weight, mix, out_weight, edge, back, energies, geometry, message)
    lax.fori_loop(0, GROUPS - 1, step, 0)


def late_kernel(
    known, up, across, early, weight, mix, out_weight,
    energy_out, spread_out, table, edge, back,
    energies, geometry, message,
):
    table[0:64] = known[192:256]
    for m in range(10):
        for y in range(2):
            fill(table, 2 + y, m, [up[1, y, m], across[0, y, m], up[0, y, m], across[1, y, m]])
    group_forward(table, weight, mix, out_weight, edge, back, energies, geometry, message)(0, 0)
    total = jnp.concatenate([early[...], energies[...]], axis=0)
    total = jnp.sum(total.T, axis=0, keepdims=True)
    energy_out[...] = jnp.broadcast_to(total, energy_out.shape)
    spread_out[...] = jnp.broadcast_to(total[None], spread_out.shape)


def stage_kernel(own, shared, own_copy, weight, mix, out_weight):
    own_copy[...] = own[...]
    weight[...] = shared[0:7]
    out_weight[...] = shared[7, 0:1]
    mix[...] = shared[8:24].reshape(C, C).astype(BF16)


def relay_kernel(gathered, out):
    total = jnp.sum(gathered[...], axis=0, keepdims=True)
    out[...] = jnp.broadcast_to(total, out.shape)


def group_backward(table, edge, back, weight, values, near, ahead):
    def backward(q, carry):
        block = block_of(q)
        first = table[block, 0:C]
        spot = pl.ds(pl.multiple_of((q + ahead) * ROWS, ROWS), ROWS)

        def spread(g, path):
            return jnp.concatenate(
                [(weight[path, b : b + 1, :] * back[q, g]).astype(BF16) for b in range(NB)], axis=0
            )

        wide = jnp.concatenate([spread(0, 0)] + [spread(g, PLAIN[g - 1]) for g in range(1, 9)], axis=1)
        grads = lax.dot_general(wide, table[block, 0 : 9 * C], NT, preferred_element_type=F32)
        along = [None] * NB
        sums = [None] * 9
        for b in range(NB):
            along[b] = grads[ROWS * b : ROWS * b + ROWS]
        paired = {1: spread(0, 1), 2: spread(0, 2)}
        for g in range(1, 9):
            both = jnp.concatenate([first, table[block, C * g : C * g + C]], axis=1)
            wide = jnp.concatenate([spread(g, LEAD[g]), paired[PAIRED[g - 1]]], axis=1)
            grads = lax.dot_general(wide, both, NT, preferred_element_type=F32)
            harmonic = edge[q, g]
            total = None
            for b in range(NB):
                part = grads[ROWS * b : ROWS * b + ROWS]
                along[b] = along[b] + part * harmonic
                term = part * edge[q, 9 + b]
                total = term if total is None else total + term
            sums[g] = total
        radial = None
        for b in range(NB):
            term = along[b] * edge[q, 17 + b]
            radial = term if radial is None else radial + term
        inv = edge[q, 0]
        ux, uy, uz = (edge[q, g] * (1.0 / R3) for g in (1, 2, 3))
        vx = R3 * sums[1] + R15 * (uy * sums[4] + uz * sums[7] + ux * sums[8])
        vy = R3 * sums[2] + R15 * (ux * sums[4] + uz * sums[5] - uy * sums[8])
        vz = R3 * sums[3] + R15 * (uy * sums[5] + ux * sums[7]) + (3.0 * R5) * uz * sums[6]
        inward = radial - inv * (ux * vx + uy * vy + uz * vz)
        for axis, (v, unit) in enumerate(((vx, ux), (vy, uy), (vz, uz))):
            gradient = inward * unit + inv * v
            values[axis, spot] = gradient
            near[axis, pl.ds(q + ahead, 1)] = jnp.sum(gradient, axis=0, keepdims=True)
        return carry

    return backward


def backward_kernel(
    table, edge, back, late_table, late_edge, late_back, weight, energy,
    near_out, send_up, values, near,
):
    near[...] = jnp.zeros_like(near)
    lax.fori_loop(0, GROUPS - 1, group_backward(table, edge, back, weight, values, near, 0), 0)
    group_backward(late_table, late_edge, late_back, weight, values, near, GROUPS - 1)(0, 0)
    send_up[...] = jnp.zeros_like(send_up)
    near_out[...] = jnp.zeros_like(near_out)
    lane = lax.broadcasted_iota(jnp.int32, (8, C), 1)
    for kind in range(4):
        if kind < 3:
            part = near[kind]
            later = pltpu.roll(pltpu.roll(part, 64, 1), 1, 0)
            pairs = -(part + later)
            own = jnp.sum(values[kind].T, axis=0, keepdims=True)
        else:
            pairs = jnp.zeros((8, C), F32)
            own = energy[0:1]
        own = jnp.concatenate(
            [own] + [pltpu.roll(own, C - 32 * q, 1) for q in range(1, 4)] + [jnp.zeros((4, C), F32)], axis=0
        )
        pairs = pairs + jnp.where((lane >= 32) & (lane < 48), pltpu.roll(own, 32, 1), 0.0)
        own = pltpu.roll(pltpu.roll(own, C - 16, 1), 1, 0)
        pairs = jnp.where(lane < 64, pairs + jnp.where(lane < 16, own, 0.0), 0.0)
        near_out[kind] = pairs
        send_up[kind : kind + 1] = pairs[4:5]


def fold_kernel(near, from_down, out):
    row = lax.broadcasted_iota(jnp.int32, (8, C), 0)
    for kind in range(4):
        out[kind] = near[kind] + jnp.where(row == 0, from_down[kind : kind + 1], 0.0)


def finish_kernel(near, from_left, forces, energies):
    for kind in range(4):
        mine, theirs = near[kind], from_left[kind]
        columns = (
            pltpu.roll(mine, C - 16, 1) + pltpu.roll(theirs, C - 8, 1),
            mine + pltpu.roll(theirs, C - 24, 1),
        )
        for x in range(2):
            for odd in range(2):
                cells = columns[x] if odd == 0 else pltpu.roll(columns[x], C - 32, 1)
                for p in range(4):
                    y = 2 * p + odd
                    if kind < 3:
                        forces[kind, x, y : y + 1] = cells[p : p + 1, 0:8]
                    else:
                        energies[x, y : y + 1] = cells[p : p + 1, 0:8]


VMEM = pl.BlockSpec(memory_space=pltpu.VMEM)


def pack_call(features, positions, occupied, neighbours, *weights):
    return pl.pallas_call(
        pack_kernel,
        out_shape=(
            jax.ShapeDtypeStruct((2, 8, 10, 8, C), BF16),
            jax.ShapeDtypeStruct((2, 2, 10, 8, C), BF16),
            jax.ShapeDtypeStruct((24, 8, C), F32),
        ),
        in_specs=[pl.BlockSpec(memory_space=pl.ANY)] * 7,
        out_specs=(VMEM,) * 3,
        scratch_shapes=[
            pltpu.VMEM(positions.shape, F32),
            pltpu.VMEM(occupied.shape, jnp.int32),
            pltpu.VMEM(neighbours.shape, jnp.int32),
            pltpu.VMEM((C, C), BF16),
            pltpu.SemaphoreType.DMA((7,)),
        ],
        name="pack",
    )(features, positions, occupied, neighbours, *weights)


def stage_call(own, shared):
    return pl.pallas_call(
        stage_kernel,
        out_shape=(
            jax.ShapeDtypeStruct(own.shape, BF16),
            jax.ShapeDtypeStruct((7, NB, C), F32),
            jax.ShapeDtypeStruct((C, C), BF16),
            jax.ShapeDtypeStruct((1, C), F32),
        ),
        in_specs=[VMEM] * 2,
        out_specs=(VMEM,) * 4,
        compiler_params=pltpu.CompilerParams(vmem_limit_bytes=8 * 1024 * 1024),
        cost_estimate=pl.CostEstimate(flops=2_000_000, bytes_accessed=2_000_000, transcendentals=0),
        name="stage",
    )(own, shared)


def results(groups, rows):
    return (
        jax.ShapeDtypeStruct((rows, 10 * C), BF16),
        jax.ShapeDtypeStruct((groups, 25, ROWS, C), F32),
        jax.ShapeDtypeStruct((groups, 9, ROWS, C), F32),
    )


SCRATCH = [pltpu.VMEM((9, NB * ROWS, C), BF16), pltpu.VMEM((9, ROWS, C), BF16)]


def early_call(*arrays):
    return pl.pallas_call(
        early_kernel,
        out_shape=(jax.ShapeDtypeStruct((3 * ROWS, C), F32),) + results(3, 256),
        in_specs=[VMEM] * 5,
        out_specs=(VMEM,) * 4,
        scratch_shapes=SCRATCH,
        compiler_params=pltpu.CompilerParams(vmem_limit_bytes=20 * 1024 * 1024),
        cost_estimate=pl.CostEstimate(flops=4_000_000_000, bytes_accessed=8_000_000, transcendentals=0),
        name="early",
    )(*arrays)


def late_call(plane, *arrays):
    return pl.pallas_call(
        late_kernel,
        out_shape=(
            jax.ShapeDtypeStruct((8, C), F32),
            jax.ShapeDtypeStruct((plane, 1, C), F32),
        ) + results(1, 128),
        in_specs=[VMEM] * 7,
        out_specs=(VMEM,) * 5,
        scratch_shapes=[pltpu.VMEM((ROWS, C), F32)] + SCRATCH,
        compiler_params=pltpu.CompilerParams(vmem_limit_bytes=20 * 1024 * 1024),
        cost_estimate=pl.CostEstimate(flops=1_000_000_000, bytes_accessed=2_000_000, transcendentals=0),
        name="late",
    )(*arrays)


def relay_call(gathered, depth):
    return pl.pallas_call(
        relay_kernel,
        out_shape=jax.ShapeDtypeStruct((depth, 1, C), F32),
        in_specs=[VMEM],
        out_specs=VMEM,
        compiler_params=pltpu.CompilerParams(vmem_limit_bytes=4 * 1024 * 1024),
        name="relay",
    )(gathered)


def backward_call(*arrays):
    return pl.pallas_call(
        backward_kernel,
        out_shape=(jax.ShapeDtypeStruct((4, 8, C), F32), jax.ShapeDtypeStruct((8, C), F32)),
        in_specs=[VMEM] * 8,
        out_specs=(VMEM,) * 2,
        scratch_shapes=[pltpu.VMEM((3, C, C), F32), pltpu.VMEM((3, 8, C), F32)],
        compiler_params=pltpu.CompilerParams(vmem_limit_bytes=20 * 1024 * 1024),
        cost_estimate=pl.CostEstimate(flops=4_000_000_000, bytes_accessed=8_000_000, transcendentals=0),
        name="backward",
    )(*arrays)


def fold_call(near, from_down):
    return pl.pallas_call(
        fold_kernel,
        out_shape=jax.ShapeDtypeStruct(near.shape, F32),
        in_specs=[VMEM] * 2,
        out_specs=VMEM,
        compiler_params=pltpu.CompilerParams(vmem_limit_bytes=4 * 1024 * 1024),
        cost_estimate=pl.CostEstimate(flops=1_000_000_000, bytes_accessed=1000, transcendentals=0),
        name="fold",
    )(near, from_down)


def finish_call(*arrays):
    return pl.pallas_call(
        finish_kernel,
        out_shape=(
            jax.ShapeDtypeStruct((3, 2, 8, 8), F32),
            jax.ShapeDtypeStruct((2, 8, 8), F32),
        ),
        in_specs=[VMEM] * 2,
        out_specs=(VMEM,) * 2,
        compiler_params=pltpu.CompilerParams(vmem_limit_bytes=4 * 1024 * 1024),
        cost_estimate=pl.CostEstimate(flops=1000, bytes_accessed=1000, transcendentals=0),
        name="finish",
    )(*arrays)


def ring(size, step):
    return [(i, (i + step) % size) for i in range(size)]


def on_device(features, positions, occupied, neighbours, radial_weight, mix_weight, out_weight, *, outer, inner):
    gy = outer + inner
    size_x = lax.axis_size("gx")
    size_y = lax.axis_size(gy)
    own, low, shared = pack_call(
        jnp.transpose(features, (0, 1, 3, 2, 4)), positions, occupied, neighbours,
        radial_weight, out_weight[None], mix_weight,
    )
    right = lax.ppermute(own, "gx", ring(size_x, -1))
    up = lax.ppermute(low, gy, ring(size_y, -1))
    corner = [
        (x * size_y + y, (x - 1) % size_x * size_y + (y - 1) % size_y)
        for x in range(size_x)
        for y in range(size_y)
    ]
    across = lax.ppermute(low, ("gx",) + gy, corner)
    own, *shared = stage_call(own, shared)
    early, *first = early_call(own, right, *shared)
    plane = size_x * lax.axis_size(outer)
    energy, spread, *last = late_call(plane, first[0], up, across, early, *shared)
    gathered = lax.all_to_all(spread, ("gx",) + outer, 0, 0)
    near, send_up = backward_call(*first, *last, shared[0], energy)
    from_down = lax.ppermute(send_up, gy, ring(size_y, 1))
    spread = relay_call(gathered, lax.axis_size(inner))
    spread, near = lax.optimization_barrier((spread, near))
    gathered = lax.all_to_all(spread, inner, 0, 0)
    near = fold_call(near, from_down)
    from_left = lax.ppermute(near, "gx", ring(size_x, 1))
    forces, slot_energy_values = finish_call(near, from_left)
    return forces, slot_energy_values, jnp.sum(gathered)


def solution(mesh):
    size_x, size_y = mesh.shape["gx"], mesh.shape["gy"]
    depth = 16 if size_y % 16 == 0 else size_y // 2
    split = Mesh(mesh.devices.reshape(size_x, size_y // depth, depth), ("gx", "gya", "gyb"))
    outer, inner = ("gya",), ("gyb",)
    gy = outer + inner
    in_specs = (
        P("gx", gy, None, None, None),
        P(None, "gx", gy, None),
        P("gx", gy, None),
        P("gx", gy, None, None),
        P(),
        P(),
        P(),
    )
    out_specs = (P(None, "gx", gy, None), P("gx", gy, None), P())

    def program(*arrays):
        return on_device(*arrays, outer=outer, inner=inner)

    return jax.shard_map(
        program, mesh=split, in_specs=in_specs, out_specs=out_specs, check_vma=False
    )
```

```python
import math

import jax
import jax.numpy as jnp
from jax import lax
from jax.experimental import pallas as pl
from jax.experimental.pallas import tpu as pltpu
from jax.sharding import Mesh, PartitionSpec as P

C = 128
NB = 8
GROUPS = 4
ROWS = 32
LEAD = (0, 3, 3, 3, 5, 5, 5, 5, 5)
PLAIN = (4, 4, 4, 6, 6, 6, 6, 6)
PAIRED = (1, 1, 1, 2, 2, 2, 2, 2)
R3 = math.sqrt(3.0)
R5 = math.sqrt(5.0)
R15 = math.sqrt(15.0)
F32 = jnp.float32
BF16 = jnp.bfloat16
NT = (((1,), (1,)), ((), ()))


def pack_kernel(
    features, places, present, lists, weight, out_weight, mix,
    out, low_out, shared, positions, occupied, neighbours, mix_copy, done,
):
    moves = [
        pltpu.make_async_copy(source, target, done.at[i])
        for i, (source, target) in enumerate(
            (
                (places, positions),
                (present, occupied),
                (lists, neighbours),
                (features, out.at[:, :, 0:9]),
                (weight, shared.at[0:7]),
                (out_weight, shared.at[7, 0:1]),
                (mix, mix_copy),
            )
        )
    ]
    for move in moves:
        move.start()
    for move in moves[:3]:
        move.wait()
    flat = [positions[axis, x] for axis in range(3) for x in range(2)]
    flat = flat + [occupied[x].astype(F32) for x in range(2)]
    flat = jnp.concatenate(flat, axis=0)
    flat = jnp.concatenate([flat, jnp.zeros((64, C - 8), F32)], axis=1)
    flat = jnp.concatenate([flat, jnp.zeros((64, C), F32)], axis=0).T[0:8]
    high = flat.astype(BF16).astype(F32)
    rest = flat - high
    middle = rest.astype(BF16).astype(F32)
    low = pltpu.roll((rest - middle), 2, 1)
    middle = pltpu.roll(middle, 1, 1)
    lane = lax.broadcasted_iota(jnp.int32, (8, C), 1)
    kind = jnp.where(lane < 64, lane & 15, 3)
    for x in range(2):
        for y in range(8):
            back = (C - (8 * x + y)) % C
            codes = jnp.concatenate(
                [jnp.zeros((8, 64), F32), neighbours[x, y].astype(F32), jnp.zeros((8, 32), F32)], axis=1
            )
            tile = jnp.where(kind == 2, pltpu.roll(low, back, 1), codes)
            tile = jnp.where(kind == 1, pltpu.roll(middle, back, 1), tile)
            tile = jnp.where(kind == 0, pltpu.roll(high, back, 1), tile)
            out[x, y, 9] = tile.astype(BF16)
    for move in moves[3:]:
        move.wait()
    shared[8:24] = mix_copy[...].astype(F32).reshape(16, 8, C)
    low_out[...] = out[:, 0:2]


def count(codes):
    lanes = lax.broadcasted_iota(jnp.int32, (ROWS, C), 1).astype(F32)
    rows = lax.broadcasted_iota(jnp.int32, (ROWS, C), 0)
    code = codes.astype(jnp.int32)
    cell = code >> 3
    step_x = (cell * 11) >> 5
    x = ((rows >> 3) & 1) + step_x
    y = (rows >> 4) + cell - 3 * step_x
    column = jnp.where(x == 0, 2, jnp.where(x == 3, 3, x - 1))
    place = jnp.where(code < 72, (y * 4 + column) * 8 + (code & 7), -1).astype(F32)
    total = jnp.zeros((ROWS, C), F32)
    for k in range(32):
        total = total + jnp.where(lanes == place[:, 64 + k : 65 + k], 1.0, 0.0)
    return total


def block_of(q):
    return pl.ds(pl.multiple_of(q * 64, 64), C)


def weighted(products, weight, path):
    total = None
    for b in range(NB):
        term = weight[path, b : b + 1, :] * products[ROWS * b : ROWS * (b + 1)]
        total = term if total is None else total + term
    return total


def group_forward(table, weight, mix, out_weight, edge, back, energies, geometry, message):
    piece = lax.broadcasted_iota(jnp.int32, (16, C), 1)
    which = lax.broadcasted_iota(jnp.int32, (16, C), 0) * 16
    pick_rows = jnp.where((which < 64) & (piece >= which) & (piece < which + 3), 1.0, 0.0).astype(BF16)
    piece = lax.broadcasted_iota(jnp.int32, (C, 4 * C), 0)
    which = (lax.broadcasted_iota(jnp.int32, (C, 4 * C), 1) >> 7) * 16
    pick_columns = jnp.where((piece >= which) & (piece < which + 3), 1.0, 0.0).astype(BF16)
    lane = lax.broadcasted_iota(jnp.int32, (1, C), 1)
    column = (lane >> 3) & 3
    place_x = jnp.where(column == 2, 0, jnp.where(column == 3, 3, column + 1))
    shift_x = place_x.astype(F32) * 5.0
    shift_y = (lane >> 5).astype(F32) * 5.0
    row = lax.broadcasted_iota(jnp.int32, (ROWS, C), 0)
    own_shift_x = ((row >> 3) & 1).astype(F32) * 5.0 + 5.0
    own_shift_y = (row >> 4).astype(F32) * 5.0 + 5.0

    def group_values(q):
        base = pl.multiple_of(q * 64, 64)
        return jnp.concatenate(
            [
                table[pl.ds(base + 32, 16), 9 * C : 10 * C],
                table[pl.ds(base + 64, 16), 9 * C : 10 * C],
            ],
            axis=0,
        )

    def forward(q, carry):
        block = block_of(q)
        around = lax.dot_general(
            pick_rows, table[block, 9 * C : 10 * C], NT, preferred_element_type=F32
        )
        mine = group_values(q)
        own_at = jnp.dot(mine, pick_columns, preferred_element_type=F32)
        rx = (around[0:1] + shift_x) - (own_at[:, 0:C] + own_shift_x)
        ry = (around[1:2] + shift_y) - (own_at[:, C : 2 * C] + own_shift_y)
        rz = around[2:3] - own_at[:, 2 * C : 3 * C]
        times = count(mine.astype(F32))
        dist_sq = rx * rx + ry * ry + rz * rz
        inside = (times > 0.5) & (dist_sq < 25.0)
        dist_sq = jnp.where(inside, dist_sq, 25.0)
        fall = jnp.where(inside, 1.0 - dist_sq * 0.04, 0.0)
        inv = lax.rsqrt(dist_sq)
        inv = inv * (1.5 - 0.5 * dist_sq * inv * inv)
        turn = dist_sq * inv * (math.pi / 5.0) - math.pi / 2.0
        sq = turn * turn
        cosine = jnp.full_like(sq, 1.0 / math.factorial(12))
        for order in (10, 8, 6, 4, 2, 0):
            sign = 1.0 if order % 4 == 0 else -1.0
            cosine = cosine * sq + sign / math.factorial(order)
        sine = jnp.full_like(sq, 1.0 / math.factorial(13))
        for order in (11, 9, 7, 5, 3, 1):
            sign = 1.0 if order % 4 == 1 else -1.0
            sine = sine * sq + sign / math.factorial(order)
        s_now, c_now = cosine, -sine * turn
        twice = 2.0 * c_now
        s_last, c_last = jnp.zeros_like(sq), jnp.ones_like(sq)
        amount = times * around[3:4]
        base = amount * fall * fall * inv
        slope = -(amount * fall) * (fall * inv * inv + 0.16)
        ux, uy, uz = rx * inv, ry * inv, rz * inv
        harmonics = (
            None,
            R3 * ux,
            R3 * uy,
            R3 * uz,
            R15 * ux * uy,
            R15 * uy * uz,
            (0.5 * R5) * (3.0 * uz * uz - 1.0),
            R15 * ux * uz,
            (0.5 * R15) * (ux * ux - uy * uy),
        )
        edge[q, 0] = inv
        for g in range(1, 9):
            edge[q, g] = harmonics[g]
        for b in range(NB):
            radial = s_now * base
            edge[q, 9 + b] = radial
            edge[q, 17 + b] = c_now * base * ((b + 1) * math.pi / 5.0) + s_now * slope
            spot = slice(ROWS * b, ROWS * b + ROWS)
            geometry[0, spot] = radial.astype(BF16)
            for g in range(1, 9):
                geometry[g, spot] = (radial * harmonics[g]).astype(BF16)
            s_now, s_last = twice * s_now - s_last, s_now
            c_now, c_last = twice * c_now - c_last, c_now
        messages = [None] * 9
        for m in (0, 2, 4, 6, 8):
            width = 1 if m == 8 else 2
            products = jnp.dot(
                geometry[0], table[block, C * m : C * (m + width)], preferred_element_type=F32
            )
            for j in range(width):
                path = 0 if m + j == 0 else PLAIN[m + j - 1]
                messages[m + j] = weighted(products[:, C * j : C * j + C], weight, path)
        first = table[block, 0:C]
        for g in range(1, 9):
            both = jnp.concatenate([first, table[block, C * g : C * g + C]], axis=1)
            products = jnp.dot(geometry[g], both, preferred_element_type=F32)
            messages[g] = messages[g] + weighted(products[:, :C], weight, LEAD[g])
            messages[0] = messages[0] + weighted(products[:, C:], weight, PAIRED[g - 1])
        for g in range(9):
            message[g] = messages[g].astype(BF16)
        mixed = jnp.dot(message[...].reshape(9 * ROWS, C), mix[...], preferred_element_type=F32)
        mixed = mixed.reshape(9, ROWS, C)
        z = mixed[0]
        for g in range(1, 9):
            z = z + mixed[g] * mixed[g]
        gate = 1.0 / (1.0 + jnp.exp(-z))
        scale = own_at[:, 3 * C : 4 * C] * out_weight[0:1]
        spot = pl.ds(pl.multiple_of(q * ROWS, ROWS), ROWS)
        energies[spot] = scale * (z * gate)
        grad = scale * gate * (1.0 + z * (1.0 - gate))
        message[0] = grad.astype(BF16)
        grad = 2.0 * grad
        for g in range(1, 9):
            message[g] = (grad * mixed[g]).astype(BF16)
        returned = lax.dot_general(
            message[...].reshape(9 * ROWS, C), mix[...], NT, preferred_element_type=F32
        )
        back[q] = returned.reshape(9, ROWS, C)
        return carry

    return forward


def fill(table, row, m, tiles):
    rows = jnp.concatenate([tile.astype(F32) for tile in tiles], axis=0)
    table[32 * row : 32 * row + 32, C * m : C * m + C] = rows.astype(BF16)


def early_kernel(own, right, weight, mix, out_weight, energies, table, edge, back, geometry, message):
    for m in range(10):
        for y in range(8):
            fill(table, y, m, [own[1, y, m], right[0, y, m], own[0, y, m], right[1, y, m]])
    step = group_forward(table, weight, mix, out_weight, edge, back, energies, geometry, message)
    lax.fori_loop(0, GROUPS - 1, step, 0)


def late_kernel(
    known, across, up, early, weight, mix, out_weight,
    energy_out, spread_out, table, edge, back,
    energies, geometry, message,
):
    table[0:64] = known[192:256]
    for m in range(10):
        for y in range(2):
            fill(table, 2 + y, m, [up[1, y, m], across[0, y, m], up[0, y, m], across[1, y, m]])
    group_forward(table, weight, mix, out_weight, edge, back, energies, geometry, message)(0, 0)
    total = jnp.concatenate([early[...], energies[...]], axis=0)
    total = jnp.sum(total.T, axis=0, keepdims=True)
    energy_out[...] = jnp.broadcast_to(total, energy_out.shape)
    spread_out[...] = jnp.broadcast_to(total[None], spread_out.shape)


def stage_kernel(own, shared, own_copy, weight, mix, out_weight):
    own_copy[...] = own[...]
    weight[...] = shared[0:7]
    out_weight[...] = shared[7, 0:1]
    mix[...] = shared[8:24].reshape(C, C).astype(BF16)


def relay_kernel(gathered, out):
    total = jnp.sum(gathered[...], axis=0, keepdims=True)
    out[...] = jnp.broadcast_to(total, out.shape)


def group_backward(table, edge, back, weight, values, near, ahead):
    def backward(q, carry):
        block = block_of(q)
        first = table[block, 0:C]
        spot = pl.ds(pl.multiple_of((q + ahead) * ROWS, ROWS), ROWS)

        def spread(g, path):
            return jnp.concatenate(
                [(weight[path, b : b + 1, :] * back[q, g]).astype(BF16) for b in range(NB)], axis=0
            )

        wide = jnp.concatenate([spread(0, 0)] + [spread(g, PLAIN[g - 1]) for g in range(1, 9)], axis=1)
        grads = lax.dot_general(wide, table[block, 0 : 9 * C], NT, preferred_element_type=F32)
        along = [None] * NB
        sums = [None] * 9
        for b in range(NB):
            along[b] = grads[ROWS * b : ROWS * b + ROWS]
        paired = {1: spread(0, 1), 2: spread(0, 2)}
        for g in range(1, 9):
            both = jnp.concatenate([first, table[block, C * g : C * g + C]], axis=1)
            wide = jnp.concatenate([spread(g, LEAD[g]), paired[PAIRED[g - 1]]], axis=1)
            grads = lax.dot_general(wide, both, NT, preferred_element_type=F32)
            harmonic = edge[q, g]
            total = None
            for b in range(NB):
                part = grads[ROWS * b : ROWS * b + ROWS]
                along[b] = along[b] + part * harmonic
                term = part * edge[q, 9 + b]
                total = term if total is None else total + term
            sums[g] = total
        radial = None
        for b in range(NB):
            term = along[b] * edge[q, 17 + b]
            radial = term if radial is None else radial + term
        inv = edge[q, 0]
        ux, uy, uz = (edge[q, g] * (1.0 / R3) for g in (1, 2, 3))
        vx = R3 * sums[1] + R15 * (uy * sums[4] + uz * sums[7] + ux * sums[8])
        vy = R3 * sums[2] + R15 * (ux * sums[4] + uz * sums[5] - uy * sums[8])
        vz = R3 * sums[3] + R15 * (uy * sums[5] + ux * sums[7]) + (3.0 * R5) * uz * sums[6]
        inward = radial - inv * (ux * vx + uy * vy + uz * vz)
        for axis, (v, unit) in enumerate(((vx, ux), (vy, uy), (vz, uz))):
            gradient = inward * unit + inv * v
            values[axis, spot] = gradient
            near[axis, pl.ds(q + ahead, 1)] = jnp.sum(gradient, axis=0, keepdims=True)
        return carry

    return backward


def backward_kernel(
    table, edge, back, late_table, late_edge, late_back, weight, energy,
    near_out, send_up, values, near,
):
    near[...] = jnp.zeros_like(near)
    lax.fori_loop(0, GROUPS - 1, group_backward(table, edge, back, weight, values, near, 0), 0)
    group_backward(late_table, late_edge, late_back, weight, values, near, GROUPS - 1)(0, 0)
    send_up[...] = jnp.zeros_like(send_up)
    near_out[...] = jnp.zeros_like(near_out)
    lane = lax.broadcasted_iota(jnp.int32, (8, C), 1)
    for kind in range(4):
        if kind < 3:
            part = near[kind]
            later = pltpu.roll(pltpu.roll(part, 64, 1), 1, 0)
            pairs = -(part + later)
            own = jnp.sum(values[kind].T, axis=0, keepdims=True)
        else:
            pairs = jnp.zeros((8, C), F32)
            own = energy[0:1]
        own = jnp.concatenate(
            [own] + [pltpu.roll(own, C - 32 * q, 1) for q in range(1, 4)] + [jnp.zeros((4, C), F32)], axis=0
        )
        pairs = pairs + jnp.where((lane >= 32) & (lane < 48), pltpu.roll(own, 32, 1), 0.0)
        own = pltpu.roll(pltpu.roll(own, C - 16, 1), 1, 0)
        pairs = jnp.where(lane < 64, pairs + jnp.where(lane < 16, own, 0.0), 0.0)
        near_out[kind] = pairs
        send_up[kind : kind + 1] = pairs[4:5]


def fold_kernel(near, from_down, out):
    row = lax.broadcasted_iota(jnp.int32, (8, C), 0)
    for kind in range(4):
        out[kind] = near[kind] + jnp.where(row == 0, from_down[kind : kind + 1], 0.0)


def finish_kernel(near, from_left, forces, energies):
    for kind in range(4):
        mine, theirs = near[kind], from_left[kind]
        columns = (
            pltpu.roll(mine, C - 16, 1) + pltpu.roll(theirs, C - 8, 1),
            mine + pltpu.roll(theirs, C - 24, 1),
        )
        for x in range(2):
            for odd in range(2):
                cells = columns[x] if odd == 0 else pltpu.roll(columns[x], C - 32, 1)
                for p in range(4):
                    y = 2 * p + odd
                    if kind < 3:
                        forces[kind, x, y : y + 1] = cells[p : p + 1, 0:8]
                    else:
                        energies[x, y : y + 1] = cells[p : p + 1, 0:8]


VMEM = pl.BlockSpec(memory_space=pltpu.VMEM)


def pack_call(features, positions, occupied, neighbours, *weights):
    return pl.pallas_call(
        pack_kernel,
        out_shape=(
            jax.ShapeDtypeStruct((2, 8, 10, 8, C), BF16),
            jax.ShapeDtypeStruct((2, 2, 10, 8, C), BF16),
            jax.ShapeDtypeStruct((24, 8, C), F32),
        ),
        in_specs=[pl.BlockSpec(memory_space=pl.ANY)] * 7,
        out_specs=(VMEM,) * 3,
        scratch_shapes=[
            pltpu.VMEM(positions.shape, F32),
            pltpu.VMEM(occupied.shape, jnp.int32),
            pltpu.VMEM(neighbours.shape, jnp.int32),
            pltpu.VMEM((C, C), BF16),
            pltpu.SemaphoreType.DMA((7,)),
        ],
        name="pack",
    )(features, positions, occupied, neighbours, *weights)


def stage_call(own, shared):
    return pl.pallas_call(
        stage_kernel,
        out_shape=(
            jax.ShapeDtypeStruct(own.shape, BF16),
            jax.ShapeDtypeStruct((7, NB, C), F32),
            jax.ShapeDtypeStruct((C, C), BF16),
            jax.ShapeDtypeStruct((1, C), F32),
        ),
        in_specs=[VMEM] * 2,
        out_specs=(VMEM,) * 4,
        compiler_params=pltpu.CompilerParams(vmem_limit_bytes=8 * 1024 * 1024),
        cost_estimate=pl.CostEstimate(flops=2_000_000, bytes_accessed=2_000_000, transcendentals=0),
        name="stage",
    )(own, shared)


def results(groups, rows):
    return (
        jax.ShapeDtypeStruct((rows, 10 * C), BF16),
        jax.ShapeDtypeStruct((groups, 25, ROWS, C), F32),
        jax.ShapeDtypeStruct((groups, 9, ROWS, C), F32),
    )


SCRATCH = [pltpu.VMEM((9, NB * ROWS, C), BF16), pltpu.VMEM((9, ROWS, C), BF16)]


def early_call(*arrays):
    return pl.pallas_call(
        early_kernel,
        out_shape=(jax.ShapeDtypeStruct((3 * ROWS, C), F32),) + results(3, 256),
        in_specs=[VMEM] * 5,
        out_specs=(VMEM,) * 4,
        scratch_shapes=SCRATCH,
        compiler_params=pltpu.CompilerParams(vmem_limit_bytes=20 * 1024 * 1024),
        cost_estimate=pl.CostEstimate(flops=4_000_000_000, bytes_accessed=8_000_000, transcendentals=0),
        name="early",
    )(*arrays)


def late_call(plane, *arrays):
    return pl.pallas_call(
        late_kernel,
        out_shape=(
            jax.ShapeDtypeStruct((8, C), F32),
            jax.ShapeDtypeStruct((plane, 1, C), F32),
        ) + results(1, 128),
        in_specs=[VMEM] * 7,
        out_specs=(VMEM,) * 5,
        scratch_shapes=[pltpu.VMEM((ROWS, C), F32)] + SCRATCH,
        compiler_params=pltpu.CompilerParams(vmem_limit_bytes=20 * 1024 * 1024),
        cost_estimate=pl.CostEstimate(flops=1_000_000_000, bytes_accessed=2_000_000, transcendentals=0),
        name="late",
    )(*arrays)


def relay_call(gathered, depth):
    return pl.pallas_call(
        relay_kernel,
        out_shape=jax.ShapeDtypeStruct((depth, 1, C), F32),
        in_specs=[VMEM],
        out_specs=VMEM,
        compiler_params=pltpu.CompilerParams(vmem_limit_bytes=4 * 1024 * 1024),
        name="relay",
    )(gathered)


def backward_call(*arrays):
    return pl.pallas_call(
        backward_kernel,
        out_shape=(jax.ShapeDtypeStruct((4, 8, C), F32), jax.ShapeDtypeStruct((8, C), F32)),
        in_specs=[VMEM] * 8,
        out_specs=(VMEM,) * 2,
        scratch_shapes=[pltpu.VMEM((3, C, C), F32), pltpu.VMEM((3, 8, C), F32)],
        compiler_params=pltpu.CompilerParams(vmem_limit_bytes=20 * 1024 * 1024),
        cost_estimate=pl.CostEstimate(flops=4_000_000_000, bytes_accessed=8_000_000, transcendentals=0),
        name="backward",
    )(*arrays)


def fold_call(near, from_down):
    return pl.pallas_call(
        fold_kernel,
        out_shape=jax.ShapeDtypeStruct(near.shape, F32),
        in_specs=[VMEM] * 2,
        out_specs=VMEM,
        compiler_params=pltpu.CompilerParams(vmem_limit_bytes=4 * 1024 * 1024),
        cost_estimate=pl.CostEstimate(flops=1_000_000_000, bytes_accessed=1000, transcendentals=0),
        name="fold",
    )(near, from_down)


def finish_call(*arrays):
    return pl.pallas_call(
        finish_kernel,
        out_shape=(
            jax.ShapeDtypeStruct((3, 2, 8, 8), F32),
            jax.ShapeDtypeStruct((2, 8, 8), F32),
        ),
        in_specs=[VMEM] * 2,
        out_specs=(VMEM,) * 2,
        compiler_params=pltpu.CompilerParams(vmem_limit_bytes=4 * 1024 * 1024),
        cost_estimate=pl.CostEstimate(flops=1000, bytes_accessed=1000, transcendentals=0),
        name="finish",
    )(*arrays)


def ring(size, step):
    return [(i, (i + step) % size) for i in range(size)]


def on_device(features, positions, occupied, neighbours, radial_weight, mix_weight, out_weight, *, outer, inner):
    gy = outer + inner
    size_x = lax.axis_size("gx")
    size_y = lax.axis_size(gy)
    own, low, shared = pack_call(
        jnp.transpose(features, (0, 1, 3, 2, 4)), positions, occupied, neighbours,
        radial_weight, out_weight[None], mix_weight,
    )
    right = lax.ppermute(own, "gx", ring(size_x, -1))
    up = lax.ppermute(low, gy, ring(size_y, -1))
    corner = [
        (x * size_y + y, (x - 1) % size_x * size_y + (y - 1) % size_y)
        for x in range(size_x)
        for y in range(size_y)
    ]
    across = lax.ppermute(low, ("gx",) + gy, corner)
    own, *shared = stage_call(own, shared)
    early, *first = early_call(own, right, *shared)
    plane = size_x * lax.axis_size(outer)
    energy, spread, *last = late_call(plane, first[0], across, up, early, *shared)
    gathered = lax.all_to_all(spread, ("gx",) + outer, 0, 0)
    near, send_up = backward_call(*first, *last, shared[0], energy)
    from_down = lax.ppermute(send_up, gy, ring(size_y, 1))
    spread = relay_call(gathered, lax.axis_size(inner))
    spread, near = lax.optimization_barrier((spread, near))
    gathered = lax.all_to_all(spread, inner, 0, 0)
    near = fold_call(near, from_down)
    from_left = lax.ppermute(near, "gx", ring(size_x, 1))
    forces, slot_energy_values = finish_call(near, from_left)
    return forces, slot_energy_values, jnp.sum(gathered)


def solution(mesh):
    size_x, size_y = mesh.shape["gx"], mesh.shape["gy"]
    depth = 16 if size_y % 16 == 0 else size_y // 2
    split = Mesh(mesh.devices.reshape(size_x, size_y // depth, depth), ("gx", "gya", "gyb"))
    outer, inner = ("gya",), ("gyb",)
    gy = outer + inner
    in_specs = (
        P("gx", gy, None, None, None),
        P(None, "gx", gy, None),
        P("gx", gy, None),
        P("gx", gy, None, None),
        P(),
        P(),
        P(),
    )
    out_specs = (P(None, "gx", gy, None), P("gx", gy, None), P())

    def program(*arrays):
        return on_device(*arrays, outer=outer, inner=inner)

    return jax.shard_map(
        program, mesh=split, in_specs=in_specs, out_specs=out_specs, check_vma=False
    )
```

```python
import math

import jax
import jax.numpy as jnp
from jax import lax
from jax.experimental import pallas as pl
from jax.experimental.pallas import tpu as pltpu
from jax.sharding import Mesh, PartitionSpec as P

C = 128
NB = 8
GROUPS = 4
ROWS = 32
LEAD = (0, 3, 3, 3, 5, 5, 5, 5, 5)
PLAIN = (4, 4, 4, 6, 6, 6, 6, 6)
PAIRED = (1, 1, 1, 2, 2, 2, 2, 2)
R3 = math.sqrt(3.0)
R5 = math.sqrt(5.0)
R15 = math.sqrt(15.0)
F32 = jnp.float32
BF16 = jnp.bfloat16
NT = (((1,), (1,)), ((), ()))


def pack_kernel(
    features, places, present, lists, weight, out_weight, mix,
    out, low_out, shared, positions, occupied, neighbours, mix_copy, done,
):
    moves = [
        pltpu.make_async_copy(source, target, done.at[i])
        for i, (source, target) in enumerate(
            (
                (places, positions),
                (present, occupied),
                (lists, neighbours),
                (features, out.at[:, :, 0:9]),
                (weight, shared.at[0:7]),
                (out_weight, shared.at[7, 0:1]),
                (mix, mix_copy),
            )
        )
    ]
    for move in moves:
        move.start()
    for move in moves[:3]:
        move.wait()
    flat = [positions[axis, x] for axis in range(3) for x in range(2)]
    flat = flat + [occupied[x].astype(F32) for x in range(2)]
    flat = jnp.concatenate(flat, axis=0)
    flat = jnp.concatenate([flat, jnp.zeros((64, C - 8), F32)], axis=1)
    flat = jnp.concatenate([flat, jnp.zeros((64, C), F32)], axis=0).T[0:8]
    high = flat.astype(BF16).astype(F32)
    rest = flat - high
    middle = rest.astype(BF16).astype(F32)
    low = pltpu.roll((rest - middle), 2, 1)
    middle = pltpu.roll(middle, 1, 1)
    lane = lax.broadcasted_iota(jnp.int32, (8, C), 1)
    kind = jnp.where(lane < 64, lane & 15, 3)
    for x in range(2):
        for y in range(8):
            back = (C - (8 * x + y)) % C
            codes = jnp.concatenate(
                [jnp.zeros((8, 64), F32), neighbours[x, y].astype(F32), jnp.zeros((8, 32), F32)], axis=1
            )
            tile = jnp.where(kind == 2, pltpu.roll(low, back, 1), codes)
            tile = jnp.where(kind == 1, pltpu.roll(middle, back, 1), tile)
            tile = jnp.where(kind == 0, pltpu.roll(high, back, 1), tile)
            out[x, y, 9] = tile.astype(BF16)
    for move in moves[3:]:
        move.wait()
    shared[8:24] = mix_copy[...].astype(F32).reshape(16, 8, C)
    low_out[...] = out[:, 0:2]


def count(codes):
    lanes = lax.broadcasted_iota(jnp.int32, (ROWS, C), 1).astype(F32)
    rows = lax.broadcasted_iota(jnp.int32, (ROWS, C), 0)
    code = codes.astype(jnp.int32)
    cell = code >> 3
    step_x = (cell * 11) >> 5
    x = ((rows >> 3) & 1) + step_x
    y = (rows >> 4) + cell - 3 * step_x
    column = jnp.where(x == 0, 2, jnp.where(x == 3, 3, x - 1))
    place = jnp.where(code < 72, (y * 4 + column) * 8 + (code & 7), -1).astype(F32)
    total = jnp.zeros((ROWS, C), F32)
    for k in range(32):
        total = total + jnp.where(lanes == place[:, 64 + k : 65 + k], 1.0, 0.0)
    return total


def block_of(q):
    return pl.ds(pl.multiple_of(q * 64, 64), C)


def weighted(products, weight, path):
    total = None
    for b in range(NB):
        term = weight[path, b : b + 1, :] * products[ROWS * b : ROWS * (b + 1)]
        total = term if total is None else total + term
    return total


def group_forward(table, weight, mix, out_weight, edge, back, energies, geometry, message):
    piece = lax.broadcasted_iota(jnp.int32, (16, C), 1)
    which = lax.broadcasted_iota(jnp.int32, (16, C), 0) * 16
    pick_rows = jnp.where((which < 64) & (piece >= which) & (piece < which + 3), 1.0, 0.0).astype(BF16)
    piece = lax.broadcasted_iota(jnp.int32, (C, 4 * C), 0)
    which = (lax.broadcasted_iota(jnp.int32, (C, 4 * C), 1) >> 7) * 16
    pick_columns = jnp.where((piece >= which) & (piece < which + 3), 1.0, 0.0).astype(BF16)
    lane = lax.broadcasted_iota(jnp.int32, (1, C), 1)
    column = (lane >> 3) & 3
    place_x = jnp.where(column == 2, 0, jnp.where(column == 3, 3, column + 1))
    shift_x = place_x.astype(F32) * 5.0
    shift_y = (lane >> 5).astype(F32) * 5.0
    row = lax.broadcasted_iota(jnp.int32, (ROWS, C), 0)
    own_shift_x = ((row >> 3) & 1).astype(F32) * 5.0 + 5.0
    own_shift_y = (row >> 4).astype(F32) * 5.0 + 5.0

    def group_values(q):
        base = pl.multiple_of(q * 64, 64)
        return jnp.concatenate(
            [
                table[pl.ds(base + 32, 16), 9 * C : 10 * C],
                table[pl.ds(base + 64, 16), 9 * C : 10 * C],
            ],
            axis=0,
        )

    def forward(q, carry):
        block = block_of(q)
        around = lax.dot_general(
            pick_rows, table[block, 9 * C : 10 * C], NT, preferred_element_type=F32
        )
        mine = group_values(q)
        own_at = jnp.dot(mine, pick_columns, preferred_element_type=F32)
        rx = (around[0:1] + shift_x) - (own_at[:, 0:C] + own_shift_x)
        ry = (around[1:2] + shift_y) - (own_at[:, C : 2 * C] + own_shift_y)
        rz = around[2:3] - own_at[:, 2 * C : 3 * C]
        times = count(mine.astype(F32))
        dist_sq = rx * rx + ry * ry + rz * rz
        inside = (times > 0.5) & (dist_sq < 25.0)
        dist_sq = jnp.where(inside, dist_sq, 25.0)
        fall = jnp.where(inside, 1.0 - dist_sq * 0.04, 0.0)
        inv = lax.rsqrt(dist_sq)
        inv = inv * (1.5 - 0.5 * dist_sq * inv * inv)
        turn = dist_sq * inv * (math.pi / 5.0) - math.pi / 2.0
        sq = turn * turn
        cosine = jnp.full_like(sq, 1.0 / math.factorial(12))
        for order in (10, 8, 6, 4, 2, 0):
            sign = 1.0 if order % 4 == 0 else -1.0
            cosine = cosine * sq + sign / math.factorial(order)
        sine = jnp.full_like(sq, 1.0 / math.factorial(13))
        for order in (11, 9, 7, 5, 3, 1):
            sign = 1.0 if order % 4 == 1 else -1.0
            sine = sine * sq + sign / math.factorial(order)
        s_now, c_now = cosine, -sine * turn
        twice = 2.0 * c_now
        s_last, c_last = jnp.zeros_like(sq), jnp.ones_like(sq)
        amount = times * around[3:4]
        base = amount * fall * fall * inv
        slope = -(amount * fall) * (fall * inv * inv + 0.16)
        ux, uy, uz = rx * inv, ry * inv, rz * inv
        harmonics = (
            None,
            R3 * ux,
            R3 * uy,
            R3 * uz,
            R15 * ux * uy,
            R15 * uy * uz,
            (0.5 * R5) * (3.0 * uz * uz - 1.0),
            R15 * ux * uz,
            (0.5 * R15) * (ux * ux - uy * uy),
        )
        edge[q, 0] = inv
        for g in range(1, 9):
            edge[q, g] = harmonics[g]
        for b in range(NB):
            radial = s_now * base
            edge[q, 9 + b] = radial
            edge[q, 17 + b] = c_now * base * ((b + 1) * math.pi / 5.0) + s_now * slope
            spot = slice(ROWS * b, ROWS * b + ROWS)
            geometry[0, spot] = radial.astype(BF16)
            for g in range(1, 9):
                geometry[g, spot] = (radial * harmonics[g]).astype(BF16)
            s_now, s_last = twice * s_now - s_last, s_now
            c_now, c_last = twice * c_now - c_last, c_now
        messages = [None] * 9
        for m in (0, 2, 4, 6, 8):
            width = 1 if m == 8 else 2
            products = jnp.dot(
                geometry[0], table[block, C * m : C * (m + width)], preferred_element_type=F32
            )
            for j in range(width):
                path = 0 if m + j == 0 else PLAIN[m + j - 1]
                messages[m + j] = weighted(products[:, C * j : C * j + C], weight, path)
        first = table[block, 0:C]
        for g in range(1, 9):
            both = jnp.concatenate([first, table[block, C * g : C * g + C]], axis=1)
            products = jnp.dot(geometry[g], both, preferred_element_type=F32)
            messages[g] = messages[g] + weighted(products[:, :C], weight, LEAD[g])
            messages[0] = messages[0] + weighted(products[:, C:], weight, PAIRED[g - 1])
        for g in range(9):
            message[g] = messages[g].astype(BF16)
        mixed = jnp.dot(message[...].reshape(9 * ROWS, C), mix[...], preferred_element_type=F32)
        mixed = mixed.reshape(9, ROWS, C)
        z = mixed[0]
        for g in range(1, 9):
            z = z + mixed[g] * mixed[g]
        gate = 1.0 / (1.0 + jnp.exp(-z))
        scale = own_at[:, 3 * C : 4 * C] * out_weight[0:1]
        spot = pl.ds(pl.multiple_of(q * ROWS, ROWS), ROWS)
        energies[spot] = scale * (z * gate)
        grad = scale * gate * (1.0 + z * (1.0 - gate))
        message[0] = grad.astype(BF16)
        grad = 2.0 * grad
        for g in range(1, 9):
            message[g] = (grad * mixed[g]).astype(BF16)
        returned = lax.dot_general(
            message[...].reshape(9 * ROWS, C), mix[...], NT, preferred_element_type=F32
        )
        back[q] = returned.reshape(9, ROWS, C)
        return carry

    return forward


def fill(table, row, m, tiles):
    rows = jnp.concatenate([tile.astype(F32) for tile in tiles], axis=0)
    table[32 * row : 32 * row + 32, C * m : C * m + C] = rows.astype(BF16)


def early_kernel(own, right, weight, mix, out_weight, energies, table, edge, back, geometry, message):
    for m in range(10):
        for y in range(8):
            fill(table, y, m, [own[1, y, m], right[0, y, m], own[0, y, m], right[1, y, m]])
    for q in range(GROUPS - 1):
        group_forward(
            table, weight, mix, out_weight, edge, back, energies, geometry.at[q], message.at[q]
        )(q, 0)


def late_kernel(
    known, up, across, early, weight, mix, out_weight,
    energy_out, spread_out, table, edge, back,
    energies, geometry, message,
):
    table[0:64] = known[192:256]
    for m in range(10):
        for y in range(2):
            fill(table, 2 + y, m, [up[1, y, m], across[0, y, m], up[0, y, m], across[1, y, m]])
    group_forward(table, weight, mix, out_weight, edge, back, energies, geometry, message)(0, 0)
    total = jnp.concatenate([early[...], energies[...]], axis=0)
    total = jnp.sum(total.T, axis=0, keepdims=True)
    energy_out[...] = jnp.broadcast_to(total, energy_out.shape)
    spread_out[...] = jnp.broadcast_to(total[None], spread_out.shape)


def stage_kernel(own, shared, own_copy, weight, mix, out_weight):
    own_copy[...] = own[...]
    weight[...] = shared[0:7]
    out_weight[...] = shared[7, 0:1]
    mix[...] = shared[8:24].reshape(C, C).astype(BF16)


def relay_kernel(gathered, out):
    total = jnp.sum(gathered[...], axis=0, keepdims=True)
    out[...] = jnp.broadcast_to(total, out.shape)


def group_backward(table, edge, back, weight, values, near, ahead):
    def backward(q, carry):
        block = block_of(q)
        first = table[block, 0:C]
        spot = pl.ds(pl.multiple_of((q + ahead) * ROWS, ROWS), ROWS)

        def spread(g, path):
            return jnp.concatenate(
                [(weight[path, b : b + 1, :] * back[q, g]).astype(BF16) for b in range(NB)], axis=0
            )

        wide = jnp.concatenate([spread(0, 0)] + [spread(g, PLAIN[g - 1]) for g in range(1, 9)], axis=1)
        grads = lax.dot_general(wide, table[block, 0 : 9 * C], NT, preferred_element_type=F32)
        along = [None] * NB
        sums = [None] * 9
        for b in range(NB):
            along[b] = grads[ROWS * b : ROWS * b + ROWS]
        paired = {1: spread(0, 1), 2: spread(0, 2)}
        for g in range(1, 9):
            both = jnp.concatenate([first, table[block, C * g : C * g + C]], axis=1)
            wide = jnp.concatenate([spread(g, LEAD[g]), paired[PAIRED[g - 1]]], axis=1)
            grads = lax.dot_general(wide, both, NT, preferred_element_type=F32)
            harmonic = edge[q, g]
            total = None
            for b in range(NB):
                part = grads[ROWS * b : ROWS * b + ROWS]
                along[b] = along[b] + part * harmonic
                term = part * edge[q, 9 + b]
                total = term if total is None else total + term
            sums[g] = total
        radial = None
        for b in range(NB):
            term = along[b] * edge[q, 17 + b]
            radial = term if radial is None else radial + term
        inv = edge[q, 0]
        ux, uy, uz = (edge[q, g] * (1.0 / R3) for g in (1, 2, 3))
        vx = R3 * sums[1] + R15 * (uy * sums[4] + uz * sums[7] + ux * sums[8])
        vy = R3 * sums[2] + R15 * (ux * sums[4] + uz * sums[5] - uy * sums[8])
        vz = R3 * sums[3] + R15 * (uy * sums[5] + ux * sums[7]) + (3.0 * R5) * uz * sums[6]
        inward = radial - inv * (ux * vx + uy * vy + uz * vz)
        for axis, (v, unit) in enumerate(((vx, ux), (vy, uy), (vz, uz))):
            gradient = inward * unit + inv * v
            values[axis, spot] = gradient
            near[axis, pl.ds(q + ahead, 1)] = jnp.sum(gradient, axis=0, keepdims=True)
        return carry

    return backward


def backward_kernel(
    table, edge, back, late_table, late_edge, late_back, weight, energy,
    near_out, send_up, values, near,
):
    near[...] = jnp.zeros_like(near)
    lax.fori_loop(0, GROUPS - 1, group_backward(table, edge, back, weight, values, near, 0), 0)
    group_backward(late_table, late_edge, late_back, weight, values, near, GROUPS - 1)(0, 0)
    send_up[...] = jnp.zeros_like(send_up)
    near_out[...] = jnp.zeros_like(near_out)
    lane = lax.broadcasted_iota(jnp.int32, (8, C), 1)
    for kind in range(4):
        if kind < 3:
            part = near[kind]
            later = pltpu.roll(pltpu.roll(part, 64, 1), 1, 0)
            pairs = -(part + later)
            own = jnp.sum(values[kind].T, axis=0, keepdims=True)
        else:
            pairs = jnp.zeros((8, C), F32)
            own = energy[0:1]
        own = jnp.concatenate(
            [own] + [pltpu.roll(own, C - 32 * q, 1) for q in range(1, 4)] + [jnp.zeros((4, C), F32)], axis=0
        )
        pairs = pairs + jnp.where((lane >= 32) & (lane < 48), pltpu.roll(own, 32, 1), 0.0)
        own = pltpu.roll(pltpu.roll(own, C - 16, 1), 1, 0)
        pairs = jnp.where(lane < 64, pairs + jnp.where(lane < 16, own, 0.0), 0.0)
        near_out[kind] = pairs
        send_up[kind : kind + 1] = pairs[4:5]


def fold_kernel(near, from_down, out):
    row = lax.broadcasted_iota(jnp.int32, (8, C), 0)
    for kind in range(4):
        out[kind] = near[kind] + jnp.where(row == 0, from_down[kind : kind + 1], 0.0)


def finish_kernel(near, from_left, forces, energies):
    for kind in range(4):
        mine, theirs = near[kind], from_left[kind]
        columns = (
            pltpu.roll(mine, C - 16, 1) + pltpu.roll(theirs, C - 8, 1),
            mine + pltpu.roll(theirs, C - 24, 1),
        )
        for x in range(2):
            for odd in range(2):
                cells = columns[x] if odd == 0 else pltpu.roll(columns[x], C - 32, 1)
                for p in range(4):
                    y = 2 * p + odd
                    if kind < 3:
                        forces[kind, x, y : y + 1] = cells[p : p + 1, 0:8]
                    else:
                        energies[x, y : y + 1] = cells[p : p + 1, 0:8]


VMEM = pl.BlockSpec(memory_space=pltpu.VMEM)


def pack_call(features, positions, occupied, neighbours, *weights):
    return pl.pallas_call(
        pack_kernel,
        out_shape=(
            jax.ShapeDtypeStruct((2, 8, 10, 8, C), BF16),
            jax.ShapeDtypeStruct((2, 2, 10, 8, C), BF16),
            jax.ShapeDtypeStruct((24, 8, C), F32),
        ),
        in_specs=[pl.BlockSpec(memory_space=pl.ANY)] * 7,
        out_specs=(VMEM,) * 3,
        scratch_shapes=[
            pltpu.VMEM(positions.shape, F32),
            pltpu.VMEM(occupied.shape, jnp.int32),
            pltpu.VMEM(neighbours.shape, jnp.int32),
            pltpu.VMEM((C, C), BF16),
            pltpu.SemaphoreType.DMA((7,)),
        ],
        name="pack",
    )(features, positions, occupied, neighbours, *weights)


def stage_call(own, shared):
    return pl.pallas_call(
        stage_kernel,
        out_shape=(
            jax.ShapeDtypeStruct(own.shape, BF16),
            jax.ShapeDtypeStruct((7, NB, C), F32),
            jax.ShapeDtypeStruct((C, C), BF16),
            jax.ShapeDtypeStruct((1, C), F32),
        ),
        in_specs=[VMEM] * 2,
        out_specs=(VMEM,) * 4,
        compiler_params=pltpu.CompilerParams(vmem_limit_bytes=8 * 1024 * 1024),
        cost_estimate=pl.CostEstimate(flops=2_000_000, bytes_accessed=2_000_000, transcendentals=0),
        name="stage",
    )(own, shared)


def results(groups, rows):
    return (
        jax.ShapeDtypeStruct((rows, 10 * C), BF16),
        jax.ShapeDtypeStruct((groups, 25, ROWS, C), F32),
        jax.ShapeDtypeStruct((groups, 9, ROWS, C), F32),
    )


SCRATCH = [pltpu.VMEM((9, NB * ROWS, C), BF16), pltpu.VMEM((9, ROWS, C), BF16)]


def early_call(*arrays):
    return pl.pallas_call(
        early_kernel,
        out_shape=(jax.ShapeDtypeStruct((3 * ROWS, C), F32),) + results(3, 256),
        in_specs=[VMEM] * 5,
        out_specs=(VMEM,) * 4,
        scratch_shapes=[
            pltpu.VMEM((3, 9, NB * ROWS, C), BF16),
            pltpu.VMEM((3, 9, ROWS, C), BF16),
        ],
        compiler_params=pltpu.CompilerParams(vmem_limit_bytes=20 * 1024 * 1024),
        cost_estimate=pl.CostEstimate(flops=4_000_000_000, bytes_accessed=8_000_000, transcendentals=0),
        name="early",
    )(*arrays)


def late_call(plane, *arrays):
    return pl.pallas_call(
        late_kernel,
        out_shape=(
            jax.ShapeDtypeStruct((8, C), F32),
            jax.ShapeDtypeStruct((plane, 1, C), F32),
        ) + results(1, 128),
        in_specs=[VMEM] * 7,
        out_specs=(VMEM,) * 5,
        scratch_shapes=[pltpu.VMEM((ROWS, C), F32)] + SCRATCH,
        compiler_params=pltpu.CompilerParams(vmem_limit_bytes=20 * 1024 * 1024),
        cost_estimate=pl.CostEstimate(flops=1_000_000_000, bytes_accessed=2_000_000, transcendentals=0),
        name="late",
    )(*arrays)


def relay_call(gathered, depth):
    return pl.pallas_call(
        relay_kernel,
        out_shape=jax.ShapeDtypeStruct((depth, 1, C), F32),
        in_specs=[VMEM],
        out_specs=VMEM,
        compiler_params=pltpu.CompilerParams(vmem_limit_bytes=4 * 1024 * 1024),
        name="relay",
    )(gathered)


def backward_call(*arrays):
    return pl.pallas_call(
        backward_kernel,
        out_shape=(jax.ShapeDtypeStruct((4, 8, C), F32), jax.ShapeDtypeStruct((8, C), F32)),
        in_specs=[VMEM] * 8,
        out_specs=(VMEM,) * 2,
        scratch_shapes=[pltpu.VMEM((3, C, C), F32), pltpu.VMEM((3, 8, C), F32)],
        compiler_params=pltpu.CompilerParams(vmem_limit_bytes=20 * 1024 * 1024),
        cost_estimate=pl.CostEstimate(flops=4_000_000_000, bytes_accessed=8_000_000, transcendentals=0),
        name="backward",
    )(*arrays)


def fold_call(near, from_down):
    return pl.pallas_call(
        fold_kernel,
        out_shape=jax.ShapeDtypeStruct(near.shape, F32),
        in_specs=[VMEM] * 2,
        out_specs=VMEM,
        compiler_params=pltpu.CompilerParams(vmem_limit_bytes=4 * 1024 * 1024),
        cost_estimate=pl.CostEstimate(flops=1_000_000_000, bytes_accessed=1000, transcendentals=0),
        name="fold",
    )(near, from_down)


def finish_call(*arrays):
    return pl.pallas_call(
        finish_kernel,
        out_shape=(
            jax.ShapeDtypeStruct((3, 2, 8, 8), F32),
            jax.ShapeDtypeStruct((2, 8, 8), F32),
        ),
        in_specs=[VMEM] * 2,
        out_specs=(VMEM,) * 2,
        compiler_params=pltpu.CompilerParams(vmem_limit_bytes=4 * 1024 * 1024),
        cost_estimate=pl.CostEstimate(flops=1000, bytes_accessed=1000, transcendentals=0),
        name="finish",
    )(*arrays)


def ring(size, step):
    return [(i, (i + step) % size) for i in range(size)]


def on_device(features, positions, occupied, neighbours, radial_weight, mix_weight, out_weight, *, outer, inner):
    gy = outer + inner
    size_x = lax.axis_size("gx")
    size_y = lax.axis_size(gy)
    own, low, shared = pack_call(
        jnp.transpose(features, (0, 1, 3, 2, 4)), positions, occupied, neighbours,
        radial_weight, out_weight[None], mix_weight,
    )
    right = lax.ppermute(own, "gx", ring(size_x, -1))
    up = lax.ppermute(low, gy, ring(size_y, -1))
    corner = [
        (x * size_y + y, (x - 1) % size_x * size_y + (y - 1) % size_y)
        for x in range(size_x)
        for y in range(size_y)
    ]
    across = lax.ppermute(low, ("gx",) + gy, corner)
    own, *shared = stage_call(own, shared)
    early, *first = early_call(own, right, *shared)
    plane = size_x * lax.axis_size(outer)
    energy, spread, *last = late_call(plane, first[0], up, across, early, *shared)
    gathered = lax.all_to_all(spread, ("gx",) + outer, 0, 0)
    near, send_up = backward_call(*first, *last, shared[0], energy)
    from_down = lax.ppermute(send_up, gy, ring(size_y, 1))
    spread = relay_call(gathered, lax.axis_size(inner))
    spread, near = lax.optimization_barrier((spread, near))
    gathered = lax.all_to_all(spread, inner, 0, 0)
    near = fold_call(near, from_down)
    from_left = lax.ppermute(near, "gx", ring(size_x, 1))
    forces, slot_energy_values = finish_call(near, from_left)
    return forces, slot_energy_values, jnp.sum(gathered)


def solution(mesh):
    size_x, size_y = mesh.shape["gx"], mesh.shape["gy"]
    depth = 16 if size_y % 16 == 0 else size_y // 2
    split = Mesh(mesh.devices.reshape(size_x, size_y // depth, depth), ("gx", "gya", "gyb"))
    outer, inner = ("gya",), ("gyb",)
    gy = outer + inner
    in_specs = (
        P("gx", gy, None, None, None),
        P(None, "gx", gy, None),
        P("gx", gy, None),
        P("gx", gy, None, None),
        P(),
        P(),
        P(),
    )
    out_specs = (P(None, "gx", gy, None), P("gx", gy, None), P())

    def program(*arrays):
        return on_device(*arrays, outer=outer, inner=inner)

    return jax.shard_map(
        program, mesh=split, in_specs=in_specs, out_specs=out_specs, check_vma=False
    )
```
